256 devices in a mesh: mem: 4 (over z_hi, core), lat: 64 (over x, y, z_lo).
Axes of the slice: x: 4, y: 4, z: 8 (z_hi: 2, z_lo: 4; z = z_hi * 4 + z_lo), core: 2. Of those that a mesh axis runs over, the one named last changes fastest.
Arguments:
- perturbations: bfloat16 [4, 2, 1280, 2560], P('mem', None, 'lat'), may hold values from -12 to 12
- row_map: int32 [1280], replicated, may hold values from 0 to 1279, each once
- wave_map: int32 [1280], replicated, may hold values from 0 to 1279, each once
- cutoffs: int32 [3], replicated, may hold values from 320 to 1120, as said below
Outputs:
- band_stats: float32 [4, 3, 1280, 2560], P(None, None, 'lat', 'mem')
- spectral_power: float32 [2, 1280, 1280], P(None, 'mem', 'lat')
The draws below stay inside these ranges and needn't reach their ends.
Inputs may be any that keep to these rules, and one draw needn't show every extreme that they name: `row_map`: each latitude row appears once. `wave_map`: each zonal wavenumber appears once. `cutoffs`: increasing; the first is 320, the last is 1120, and each exceeds the one before by 160 or more.
All inputs are finite; a program needn't handle non-finite values.
Results may differ from the reference program's by a relative error of at most 0.014.
Values may be sent and summed in bfloat16 or wider, within the bound.
No kernel may reach another device: no remote copies, remote signals or barrier semaphores. Data moves between devices by JAX's collectives and lax.ppermute only.
A program may use at most 256 MiB of HBM per device.

```python
import math
import jax
import jax.numpy as jnp
from jax import lax

NLAT = 1280
NLON = 2560
MT = 1280
NT = 1280
LEV = 2
BANDS = 4
MEMBERS = 4


def draw_cutoffs(key, part):
    key = jax.random.fold_in(key, 7)
    first = jnp.int32(NT // 4)
    second = first + NT // 8 + jax.random.randint(key, (), 0, NT // 4)
    third = jnp.int32(NT - NT // 8)
    return jnp.stack([first, second, third]).astype(jnp.int32)


def draw_perturbations(key, part):
    key = jax.random.fold_in(key, 11)
    base_key = jax.random.fold_in(key, 1)
    alternate_key = jax.random.fold_in(key, 2)
    base = jnp.clip(2.0 * jax.random.normal(base_key, (MEMBERS, LEV, NLAT, NLON), jnp.float32), -10.0, 10.0)
    amplitude = jnp.clip(jax.random.normal(alternate_key, (MEMBERS, LEV, NLAT, 1), jnp.float32), -2.0, 2.0)
    sign = 1.0 - 2.0 * (jnp.arange(NLON, dtype=jnp.int32) % 2).astype(jnp.float32)
    return (base + amplitude * sign[None, None, None, :]).astype(jnp.bfloat16)


def setup_inputs(seed: int = 0) -> dict:
    seeds = jax.random.split(jax.random.key(seed), 5)
    return {
        "perturbations": draw_perturbations(jax.random.fold_in(seeds[4], 71), 0),
        "row_map": jax.random.permutation(seeds[1], NLAT).astype(jnp.int32),
        "wave_map": jax.random.permutation(seeds[2], MT).astype(jnp.int32),
        "cutoffs": draw_cutoffs(jax.random.fold_in(seeds[4], 71), 0),
    }


def zonal_table(wavenums, lon_count):
    longitude = jnp.arange(lon_count, dtype=jnp.int32)
    product = longitude[:, None] * wavenums[None, :] % lon_count
    angle = product.astype(jnp.float32) * (2.0 * math.pi / lon_count)
    weight = jnp.where(wavenums == 0, math.sqrt(1.0 / lon_count), math.sqrt(2.0 / lon_count)).astype(jnp.float32)
    table = jnp.stack([jnp.cos(angle) * weight[None, :], jnp.sin(angle) * weight[None, :]], axis=-1)
    return table.astype(jnp.bfloat16)

def meridional_table(row_map, lat_count, wave_count):
    degree = jnp.arange(wave_count, dtype=jnp.int32)
    product = (2 * row_map[:, None] + 1) * degree[None, :] % (4 * lat_count)
    angle = product.astype(jnp.float32) * (math.pi / (2.0 * lat_count))
    weight = jnp.where(degree == 0, math.sqrt(1.0 / lat_count), math.sqrt(2.0 / lat_count)).astype(jnp.float32)
    return (jnp.cos(angle) * weight[None, :]).astype(jnp.bfloat16)

def reference(perturbations, row_map, wave_map, cutoffs):
    members = perturbations.shape[0]
    fields_count = members * LEV
    zonal = zonal_table(wave_map, NLON).reshape(NLON, 2 * MT)
    meridional = meridional_table(row_map, NLAT, NT)
    flat = perturbations.reshape(fields_count * NLAT, NLON)
    waves = jnp.dot(flat, zonal, preferred_element_type=jnp.float32).astype(jnp.bfloat16)
    waves = waves.reshape(fields_count, NLAT, 2 * MT).transpose(1, 0, 2).reshape(NLAT, fields_count * 2 * MT)
    spectra = lax.dot_general(meridional, waves, (((0,), (0,)), ((), ())), preferred_element_type=jnp.float32).astype(jnp.bfloat16)
    spectra = lax.optimization_barrier(spectra)
    spec_wide = spectra.astype(jnp.float32).reshape(NT, members, LEV, MT, 2)
    power = lax.optimization_barrier(jnp.sum(spec_wide * spec_wide, axis=(1, 4))).transpose(1, 0, 2) / (2.0 * (members - 1))
    degree = jnp.arange(NT, dtype=jnp.int32)[:, None]
    kappa = degree * degree + (wave_map * wave_map)[None, :]
    band_index = jnp.zeros((NT, MT), jnp.int32)
    for cut in range(BANDS - 1):
        band_index = band_index + (kappa >= cutoffs[cut] * cutoffs[cut]).astype(jnp.int32)
    spec_parts = spectra.reshape(NT, fields_count, MT, 2)
    results = []
    for band in range(BANDS):
        keep = (band_index == band)[:, None, :, None]
        masked = jnp.where(keep, spec_parts, jnp.zeros((), jnp.bfloat16)).reshape(NT, fields_count * 2 * MT)
        band_waves = jnp.dot(meridional, masked, preferred_element_type=jnp.float32).astype(jnp.bfloat16)
        band_waves = band_waves.reshape(NLAT, fields_count, 2 * MT).transpose(1, 0, 2).reshape(fields_count * NLAT, 2 * MT)
        fields = lax.dot_general(band_waves, zonal, (((1,), (1,)), ((), ())), preferred_element_type=jnp.float32).astype(jnp.bfloat16)
        fields = lax.optimization_barrier(fields)
        fields = fields.astype(jnp.float32).reshape(members, LEV, NLAT, NLON)
        lower_level = fields[:, 0]
        upper_level = fields[:, 1]
        results.append(jnp.stack([lax.optimization_barrier(jnp.sum(lower_level * lower_level, 0)), lax.optimization_barrier(jnp.sum(upper_level * upper_level, 0)), lax.optimization_barrier(jnp.sum(lower_level * upper_level, 0))], 0))
    band_stats = jnp.stack(results, 0) / (members - 1.0)
    return (band_stats, power)
```

```python
import functools
import math

import jax
import jax.numpy as jnp
from jax import lax
from jax.experimental import pallas as pl
from jax.experimental.pallas import tpu as pltpu
from jax.sharding import PartitionSpec as P

F32 = jnp.float32
BF16 = jnp.bfloat16
LANES = 128
ROW_PAD = 24
SENT_BANDS = 3
SINE = (
    6.283185307072579,
    -41.341702116996316,
    81.60522620630826,
    -76.70428132156577,
    42.00980565792769,
    -14.394135376685622,
)


def cos_turn(index, period):
    left = index - jnp.round(index * (1.0 / period)) * period
    quarter = 0.25 - jnp.abs(left * (1.0 / period))
    square = quarter * quarter
    total = jnp.full_like(square, SINE[-1])
    for coefficient in SINE[-2::-1]:
        total = total * square + coefficient
    return total * quarter


def cosine_rows(rate, offset, period, weight, steps):
    lane = lax.broadcasted_iota(jnp.int32, (1, LANES), 1).astype(F32)
    start = rate * lane + offset
    stride = rate * float(LANES)
    before = cos_turn(start, period) * weight
    now = cos_turn(start + stride, period) * weight
    twice = jnp.broadcast_to(2.0 * cos_turn(stride, period), before.shape)
    tiles = [before, now]
    while len(tiles) < steps:
        tiles.append(twice * tiles[-1] - tiles[-2])
    return tiles


def move_lanes(block, source, target):
    tile, inner = divmod(source, LANES)
    first = block[:, tile * LANES : (tile + 1) * LANES]
    if inner + 40 > LANES and (tile + 1) * LANES < block.shape[1]:
        second = block[:, (tile + 1) * LANES : (tile + 2) * LANES]
        lane = lax.broadcasted_iota(jnp.int32, first.shape, 1)
        first = jnp.where(lane >= inner, first, second)
    shift = (target - inner) % LANES
    return pltpu.roll(first, shift, 1) if shift else first


def join_lanes(pieces, width):
    lane = lax.broadcasted_iota(jnp.int32, pieces[0].shape, 1)
    out = jnp.zeros_like(pieces[0])
    for index in range(len(pieces) - 1, -1, -1):
        out = jnp.where(lane < (index + 1) * width, pieces[index], out)
    return out


def forward_kernel(x_ref, wave_ref, odd_ref, table_ref, out_ref, folded, total, *, lon_count, slots):
    step = pl.program_id(0)
    levels, rows, _ = x_ref.shape
    half = lon_count // 2
    block = table_ref.shape[0]

    @pl.when(step == 0)
    def _():
        folded[...] = jnp.zeros_like(folded)
        for level in range(levels):
            near = x_ref[level, :, :half].astype(F32)
            far = x_ref[level, :, half:].astype(F32)
            folded[32 * level : 32 * level + rows, :] = (near + far).astype(BF16)
            folded[64 + 32 * level : 64 + 32 * level + rows, :] = (near - far).astype(BF16)

    chunk = 64
    for start in range(0, block, chunk):
        code = wave_ref[start : start + chunk, :]
        part = lax.shift_right_logical(code, 11)
        wave = code - part * 2048
        weight = jnp.where(wave == 0, math.sqrt(1.0 / lon_count), math.sqrt(2.0 / lon_count)).astype(F32)
        offset = part.astype(F32) * (-0.25 * lon_count)
        tiles = cosine_rows(wave.astype(F32), offset, float(lon_count), weight, half // LANES)
        for index, tile in enumerate(tiles):
            table_ref[start : start + chunk, index * LANES : (index + 1) * LANES] = tile.astype(BF16)
    columns = pl.ds(pl.multiple_of(step * block, block), block)
    total[:, columns] = lax.dot_general(
        folded[...], table_ref[...], (((1,), (1,)), ((), ())), preferred_element_type=F32
    )

    @pl.when(step == pl.num_programs(0) - 1)
    def _():
        picked = jnp.where(odd_ref[...] == 1, total[64:128, :], total[0:64, :])
        width = 2 * slots
        for dest in range(out_ref.shape[0]):
            pieces = [
                move_lanes(picked[32 * level : 32 * level + ROW_PAD, :], dest * width, level * width)
                for level in range(levels)
            ]
            out_ref[dest] = join_lanes(pieces, width).astype(BF16)


def meridional_kernel(row_ref, out_ref, *, lat_count):
    block, waves = out_ref.shape
    chunk = 64
    lane = lax.broadcasted_iota(jnp.int32, (1, LANES), 1)
    for start in range(0, block, chunk):
        row = row_ref[start : start + chunk, :]
        weight = jnp.where(row < 0, 0.0, math.sqrt(2.0 / lat_count)).astype(F32)
        rate = (2 * row + 1).astype(F32)
        tiles = cosine_rows(rate, 0.0, 4.0 * lat_count, weight, waves // LANES)
        for index, tile in enumerate(tiles):
            if index == 0:
                tile = jnp.where(lane == 0, tile * math.sqrt(0.5), tile)
            out_ref[start : start + chunk, index * LANES : (index + 1) * LANES] = tile.astype(BF16)


def spectral_kernel(cut_ref, waves_ref, far_ref, own_ref, out_ref, power_ref, table_ref, arrived, *, slots):
    chunks = arrived.shape[0]
    size = table_ref.shape[0] // chunks
    copies = []
    for chunk in range(chunks):
        part = pl.ds(chunk * size, size)
        copies.append(pltpu.make_async_copy(far_ref.at[part], table_ref.at[part], arrived.at[chunk]))
        copies[-1].start()
    spectra = None
    for chunk in range(chunks):
        copies[chunk].wait()
        part = pl.ds(chunk * size, size)
        term = lax.dot_general(
            waves_ref[part], table_ref[part], (((0,), (0,)), ((), ())), preferred_element_type=F32
        )
        spectra = term if spectra is None else spectra + term
    table = table_ref[...]
    fields = 2 * slots
    count = 2 * fields
    spectra = spectra[0:count, :].astype(BF16)
    wide = spectra.astype(F32)
    square = wide * wide
    for level in range(2):
        base = level * fields
        power_ref[level] = square[base : base + slots, :] + square[base + slots : base + fields, :]
    wave = own_ref[...]
    degree = lax.broadcasted_iota(jnp.int32, wide.shape, 1)
    kappa = degree * degree + wave * wave
    below = [kappa < cut_ref[i] * cut_ref[i] for i in range(SENT_BANDS)]
    parts = []
    for band in range(SENT_BANDS):
        keep = below[band]
        if band:
            keep = jnp.logical_and(keep, jnp.logical_not(below[band - 1]))
        parts.append(jnp.where(keep, wide, 0.0).astype(BF16))
    masked = jnp.concatenate(parts, axis=0)
    band_waves = lax.dot_general(masked, table, (((1,), (1,)), ((), ())), preferred_element_type=F32)
    rows = 20
    for dest in range(out_ref.shape[0]):
        pieces = []
        for piece in range(2 * SENT_BANDS):
            part = band_waves[piece * fields : (piece + 1) * fields, :]
            pieces.append(move_lanes(part, dest * ROW_PAD, piece * rows))
        out_ref[dest] = join_lanes(pieces, rows).astype(BF16)


def inverse_kernel(
    place_ref, waves_ref, odd_ref, x_ref, far_ref, keep_ref, send_ref, table, lhs, field, arrived
):
    levels, rows, lon_count = x_ref.shape
    half = lon_count // 2
    steps, _, block = table.shape
    kept = levels * rows
    copies = []
    for step in range(steps):
        part = far_ref.at[:, pl.ds(step * block, block)]
        copies.append(pltpu.make_async_copy(part, table.at[step], arrived.at[step]))
        copies[-1].start()
    waves = jnp.transpose(waves_ref[...].astype(F32))
    flag = odd_ref[...] == 1
    lhs[0:LANES, :] = jnp.where(flag, 0.0, waves).astype(BF16)
    lhs[LANES:, :] = jnp.where(flag, waves, 0.0).astype(BF16)
    for level in range(levels):
        field[level * rows : (level + 1) * rows, :] = x_ref[level].astype(F32)
    values = field[...]
    lane = lax.broadcasted_iota(jnp.int32, values.shape, 1)
    sign = 1.0 - 2.0 * (lane % 2).astype(F32)
    mean = jnp.sum(values * sign, axis=1, keepdims=True) * (1.0 / lon_count)
    field[...] = values - mean * sign

    core = place_ref[0]
    per_block = (lon_count // 4) // LANES
    for step in range(steps):
        copies[step].wait()
        both = jnp.dot(lhs[...], table[step], preferred_element_type=F32)
        even, odd = both[:LANES], both[LANES:]
        for side in range(2):
            bands = even + odd if side == 0 else even - odd
            bands = bands.astype(BF16).astype(F32)
            base = step * block + side * half
            rest = field[:, base : base + block]
            for band in range(SENT_BANDS):
                rest = rest - bands[band * kept : (band + 1) * kept]
            full = jnp.concatenate([bands[: SENT_BANDS * kept], rest], axis=0).astype(BF16)
            for tile in range(block // LANES):
                owner, spot = divmod(step * (block // LANES) + tile, per_block)
                lanes = slice(spot * LANES, (spot + 1) * LANES)
                value = full[:, tile * LANES : (tile + 1) * LANES]

                @pl.when(core == owner)
                def _(value=value, lanes=lanes, side=side):
                    keep_ref[side, :, lanes] = value

                @pl.when(core != owner)
                def _(value=value, lanes=lanes, side=side):
                    send_ref[side, :, lanes] = value


def terms_of(first, second, rows, bands):
    a, b = first.astype(F32), second.astype(F32)
    squares = a * a + b * b
    cross = []
    for band in range(bands):
        low = band * 2 * rows
        mid, high = low + rows, low + 2 * rows
        cross.append(a[low:mid] * a[mid:high] + b[low:mid] * b[mid:high])
    return squares, cross


def pair_kernel(place_ref, keep_ref, came_ref, own_ref, send_ref, *, rows, bands):
    side = place_ref[1]
    wide = 2 * rows * bands

    def put(which, out_ref):
        squares, cross = terms_of(keep_ref[which], came_ref[which], rows, bands)
        out_ref[0:wide, :] = squares.astype(out_ref.dtype)
        out_ref[wide:, :] = jnp.concatenate(cross, axis=0).astype(out_ref.dtype)

    put(1 - side, send_ref)
    put(side, own_ref)


def final_kernel(own_ref, came_ref, out_ref, *, rows, bands, scale):
    total = (own_ref[...] + came_ref[...].astype(F32)) * scale
    wide = 2 * rows * bands
    for band in range(bands):
        low = band * 2 * rows
        out_ref[0, :, band, :] = total[low : low + rows]
        out_ref[1, :, band, :] = total[low + rows : low + 2 * rows]
        out_ref[2, :, band, :] = total[wide + band * rows : wide + (band + 1) * rows]


VMEM_LIMIT = 24 * 1024 * 1024
WIDE_LIMIT = 52_000_000
WIDER_LIMIT = 54_000_000
WHOLE = pl.BlockSpec(memory_space=pltpu.VMEM)
FAR = pl.BlockSpec(memory_space=pltpu.HBM)
SCALARS = pl.BlockSpec(memory_space=pltpu.SMEM)


def params(limit=VMEM_LIMIT):
    return pltpu.CompilerParams(vmem_limit_bytes=limit)


def shards(perturbations, row_map, wave_map, cutoffs):
    _, levels, rows, lon_count = perturbations.shape
    lat_dev = lax.axis_size("lat")
    mem_dev = lax.axis_size("mem")
    lat = lax.axis_index("lat")
    mem = lax.axis_index("mem")
    swap = lambda value, bit: lax.ppermute(value, "mem", [(i, i ^ bit) for i in range(mem_dev)])
    lat_count = rows * lat_dev
    slot_count = wave_map.shape[0]
    slots = slot_count // lat_dev
    degrees = row_map.shape[0]
    bands = cutoffs.shape[0] + 1
    half = lon_count // 2
    x = perturbations[0]

    by_dev = jnp.broadcast_to(wave_map.reshape(lat_dev, 1, slots), (lat_dev, 2, slots))
    part = lax.broadcasted_iota(jnp.int32, by_dev.shape, 1)
    wave_code = (by_dev + 2048 * part).reshape(2 * slot_count, 1)
    odd = (by_dev % 2).reshape(1, 2 * slot_count)
    columns = 2 * slot_count
    block = 256

    table, outgoing = pl.pallas_call(
        functools.partial(forward_kernel, lon_count=lon_count, slots=slots),
        grid=(columns // block,),
        in_specs=[
            pl.BlockSpec((levels, rows, lon_count), lambda i: (0, 0, 0)),
            pl.BlockSpec((block, 1), lambda i: (i, 0)),
            pl.BlockSpec((1, columns), lambda i: (0, 0)),
        ],
        out_specs=[
            pl.BlockSpec((block, half), lambda i: (i, 0)),
            pl.BlockSpec((lat_dev, ROW_PAD, LANES), lambda i: (0, 0, 0)),
        ],
        out_shape=[
            pltpu.HBM((columns, half), BF16),
            jax.ShapeDtypeStruct((lat_dev, ROW_PAD, LANES), BF16),
        ],
        scratch_shapes=[pltpu.VMEM((LANES, half), BF16), pltpu.VMEM((LANES, columns), F32)],
        compiler_params=params(),
        cost_estimate=pl.CostEstimate(flops=10**9, bytes_accessed=7 * 10**6, transcendentals=0),
        name="forward_zonal",
    )(x, wave_code, odd)

    incoming = lax.all_to_all(outgoing, "lat", 0, 0, tiled=True).reshape(lat_dev * ROW_PAD, LANES)

    row_code = jnp.pad(
        row_map.reshape(lat_dev, rows), ((0, 0), (0, ROW_PAD - rows)), constant_values=-1
    ).reshape(lat_dev * ROW_PAD, 1)
    lat_block = 512
    meridional = pl.pallas_call(
        functools.partial(meridional_kernel, lat_count=lat_count),
        grid=(lat_dev * ROW_PAD // lat_block,),
        in_specs=[pl.BlockSpec((lat_block, 1), lambda i: (i, 0))],
        out_specs=pl.BlockSpec((lat_block, degrees), lambda i: (i, 0)),
        out_shape=pltpu.HBM((lat_dev * ROW_PAD, degrees), BF16),
        compiler_params=params(),
        cost_estimate=pl.CostEstimate(flops=10**9, bytes_accessed=4 * 10**6, transcendentals=0),
        name="meridional_table",
    )(row_code)

    own = lax.dynamic_slice_in_dim(wave_map, lat * slots, slots)
    own_rows = jnp.tile(own, 4).reshape(4 * slots, 1)
    band_out, power_terms = pl.pallas_call(
        functools.partial(spectral_kernel, slots=slots),
        in_specs=[SCALARS, WHOLE, FAR, WHOLE],
        out_specs=[WHOLE, WHOLE],
        out_shape=[
            jax.ShapeDtypeStruct((lat_dev, 2 * slots, LANES), BF16),
            jax.ShapeDtypeStruct((levels, slots, degrees), F32),
        ],
        scratch_shapes=[pltpu.VMEM(meridional.shape, BF16), pltpu.SemaphoreType.DMA((6,))],
        compiler_params=params(WIDER_LIMIT),
        cost_estimate=pl.CostEstimate(flops=15 * 10**8, bytes_accessed=6 * 10**6, transcendentals=0),
        name="spectral_bands",
    )(cutoffs, incoming, meridional, own_rows)

    returned = lax.all_to_all(band_out, "lat", 0, 0, tiled=True).reshape(columns, LANES)
    core, side = mem % 2, mem // 2
    pairs = power_terms.reshape(levels, slots, 2, 2, degrees // mem_dev).transpose(3, 2, 1, 0, 4)
    other = lax.dynamic_index_in_dim(pairs, 1 - core, 0, keepdims=False).astype(BF16)
    summed = lax.dynamic_index_in_dim(pairs, core, 0, keepdims=False) + swap(other, 1).astype(F32)
    other = lax.dynamic_index_in_dim(summed, 1 - side, 0, keepdims=False).astype(BF16)
    power = lax.dynamic_index_in_dim(summed, side, 0, keepdims=False) + swap(other, 2).astype(F32)
    power = (power / (2.0 * (mem_dev - 1))).transpose(1, 2, 0)

    place = jnp.stack([core, side]).astype(jnp.int32)
    lon_dev = lon_count // mem_dev
    kept = levels * rows * bands
    lon_block = 256
    pair_shape = jax.ShapeDtypeStruct((2, kept, lon_dev), BF16)
    keep, send = pl.pallas_call(
        inverse_kernel,
        in_specs=[SCALARS, WHOLE, WHOLE, WHOLE, FAR],
        out_specs=[WHOLE, WHOLE],
        out_shape=[pair_shape, pair_shape],
        scratch_shapes=[
            pltpu.VMEM((half // lon_block, columns, lon_block), BF16),
            pltpu.VMEM((2 * LANES, columns), BF16),
            pltpu.VMEM((levels * rows, lon_count), F32),
            pltpu.SemaphoreType.DMA((half // lon_block,)),
        ],
        compiler_params=params(WIDE_LIMIT),
        cost_estimate=pl.CostEstimate(flops=2 * 10**9, bytes_accessed=9 * 10**6, transcendentals=0),
        name="inverse_zonal",
    )(place, returned, odd, x, table)

    came = swap(send, 1)
    term_rows = 3 * rows * bands
    own_terms, send_terms = pl.pallas_call(
        functools.partial(pair_kernel, rows=rows, bands=bands),
        in_specs=[SCALARS, WHOLE, WHOLE],
        out_specs=[WHOLE, WHOLE],
        out_shape=[
            jax.ShapeDtypeStruct((term_rows, lon_dev), F32),
            jax.ShapeDtypeStruct((term_rows, lon_dev), BF16),
        ],
        compiler_params=params(),
        name="pair_terms",
    )(place, keep, came)
    came_terms = swap(send_terms, 2)
    band_stats = pl.pallas_call(
        functools.partial(final_kernel, rows=rows, bands=bands, scale=1.0 / (mem_dev - 1)),
        in_specs=[WHOLE, WHOLE],
        out_specs=WHOLE,
        out_shape=jax.ShapeDtypeStruct((3, rows, bands, lon_dev), F32),
        compiler_params=params(),
        name="final_terms",
    )(own_terms, came_terms).transpose(2, 0, 1, 3)
    return (band_stats, power)


def solution(mesh):
    placed = (P("mem", None, "lat", None), P(), P(), P())
    return jax.shard_map(
        shards,
        mesh=mesh,
        in_specs=placed,
        out_specs=(P(None, None, "lat", "mem"), P(None, "mem", "lat")),
        check_vma=False,
    )
```

```python
import functools
import math

import jax
import jax.numpy as jnp
from jax import lax
from jax.experimental import pallas as pl
from jax.experimental.pallas import tpu as pltpu
from jax.sharding import PartitionSpec as P

F32 = jnp.float32
BF16 = jnp.bfloat16
LANES = 128
ROW_PAD = 24
SENT_BANDS = 3
SINE = (
    6.283185307072579,
    -41.341702116996316,
    81.60522620630826,
    -76.70428132156577,
    42.00980565792769,
    -14.394135376685622,
)


def cos_turn(index, period):
    left = index - jnp.round(index * (1.0 / period)) * period
    quarter = 0.25 - jnp.abs(left * (1.0 / period))
    square = quarter * quarter
    total = jnp.full_like(square, SINE[-1])
    for coefficient in SINE[-2::-1]:
        total = total * square + coefficient
    return total * quarter


def cosine_rows(rate, offset, period, weight, steps):
    lane = lax.broadcasted_iota(jnp.int32, (1, LANES), 1).astype(F32)
    start = rate * lane + offset
    stride = rate * float(LANES)
    before = cos_turn(start, period) * weight
    now = cos_turn(start + stride, period) * weight
    twice = jnp.broadcast_to(2.0 * cos_turn(stride, period), before.shape)
    tiles = [before, now]
    while len(tiles) < steps:
        tiles.append(twice * tiles[-1] - tiles[-2])
    return tiles


def move_lanes(block, source, target):
    tile, inner = divmod(source, LANES)
    first = block[:, tile * LANES : (tile + 1) * LANES]
    if inner + 40 > LANES and (tile + 1) * LANES < block.shape[1]:
        second = block[:, (tile + 1) * LANES : (tile + 2) * LANES]
        lane = lax.broadcasted_iota(jnp.int32, first.shape, 1)
        first = jnp.where(lane >= inner, first, second)
    shift = (target - inner) % LANES
    return pltpu.roll(first, shift, 1) if shift else first


def join_lanes(pieces, width):
    lane = lax.broadcasted_iota(jnp.int32, pieces[0].shape, 1)
    out = jnp.zeros_like(pieces[0])
    for index in range(len(pieces) - 1, -1, -1):
        out = jnp.where(lane < (index + 1) * width, pieces[index], out)
    return out


def swap_parts(block, slots):
    rows, lanes = block.shape
    split = block.reshape(rows // (2 * slots), 2 * slots, lanes)
    return pltpu.roll(split, slots, 1).reshape(rows, lanes)


def wave_rows(wave_ref, slots, rows):
    wave = jnp.broadcast_to(wave_ref[...], (rows, wave_ref.shape[1]))
    count = wave.shape[1]
    lane = lax.broadcasted_iota(jnp.int32, (rows, LANES), 1)
    tiles = []
    for tile in range(2 * count // LANES):
        total = jnp.zeros((rows, LANES), jnp.int32)
        first = tile * LANES // slots
        last = ((tile + 1) * LANES - 1) // slots
        for piece in range(first, last + 1):
            device, part = divmod(piece, 2)
            target = piece * slots - tile * LANES
            moved = move_lanes(wave, device * slots, target % LANES)
            mask = jnp.logical_and(lane >= target, lane < target + slots)
            total = jnp.where(mask, moved + 2048 * part, total)
        tiles.append(total)
    return jnp.concatenate(tiles, axis=1)


def forward_kernel(x_ref, wave_ref, table_ref, out_ref, odd_ref, folded, total, sides, held, *, slots):
    step = pl.program_id(0)
    levels, rows, lon_count = x_ref.shape
    half = lon_count // 2
    block = held.shape[0]
    period = float(lon_count)

    @pl.when(step == 0)
    def _():
        code = wave_rows(wave_ref, slots, 8)
        part = lax.shift_right_logical(code, 11)
        wave = code - part * 2048
        odd_ref[...] = wave % 2
        waved = wave.astype(F32)
        phase = part.astype(F32)
        weight = jnp.where(wave == 0, math.sqrt(1.0 / lon_count), math.sqrt(2.0 / lon_count)).astype(F32)
        turn = waved * float(LANES)
        cosine = cos_turn(turn, period)
        sine = cos_turn(turn - 0.25 * period, period) * (2.0 * phase - 1.0)
        index = lax.broadcasted_iota(jnp.int32, code.shape, 0)
        stack = jnp.where(index == 0, waved, -0.25 * period * phase)
        stack = jnp.where(index == 2, weight, stack)
        stack = jnp.where(index == 3, cosine, stack)
        stack = jnp.where(index == 4, sine, stack)
        sides[...] = jnp.transpose(stack)
        folded[...] = jnp.zeros_like(folded)
        for level in range(levels):
            near = x_ref[level, :, :half].astype(F32)
            far = x_ref[level, :, half:].astype(F32)
            folded[32 * level : 32 * level + rows, :] = (near + far).astype(BF16)
            folded[64 + 32 * level : 64 + 32 * level + rows, :] = (near - far).astype(BF16)

    lane = lax.broadcasted_iota(jnp.int32, (1, LANES), 1).astype(F32)
    chunk = 4 * slots
    def make(base, count, stores):
        for start in range(0, count, chunk):
            side = sides[pl.ds(pl.multiple_of(base + start, 8), chunk), :]
            now = cos_turn(side[:, 0:1] * lane + side[:, 1:2], period) * side[:, 2:3]
            cosine = jnp.broadcast_to(side[:, 3:4], now.shape)
            later = now * cosine + swap_parts(now, slots) * side[:, 4:5]
            twice = cosine + cosine
            for index in range(half // LANES):
                value = now.astype(BF16)
                for ref, place in stores:
                    ref[place + start : place + start + chunk, index * LANES : (index + 1) * LANES] = value
                now, later = later, twice * later - now

    def multiply(ref, place, index):
        total[index, :, :block] = lax.dot_general(
            folded[...], ref[place : place + block], (((1,), (1,)), ((), ())), preferred_element_type=F32
        )

    base = step * 2 * block
    multiply(held, 0, jnp.maximum(2 * step - 1, 0))
    make(base, block, [(table_ref, 0)])
    multiply(table_ref, 0, 2 * step)
    make(base + block, block, [(table_ref, block), (held, 0)])

    @pl.when(step == pl.num_programs(0) - 1)
    def _():
        multiply(held, 0, 2 * step + 1)
        width = 2 * slots
        share = block // width
        flags = jnp.concatenate([odd_ref[0:1, :], jnp.zeros((1, LANES), jnp.int32)], axis=1)
        for group in range(total.shape[0]):
            odd = flags[:, group * block : group * block + total.shape[2]]
            picked = jnp.where(odd == 1, total[group, 64:128, :], total[group, 0:64, :])
            for dest in range(share):
                pieces = [
                    move_lanes(picked[32 * level : 32 * level + ROW_PAD, :], dest * width, level * width)
                    for level in range(levels)
                ]
                out_ref[group * share + dest] = join_lanes(pieces, width).astype(BF16)


def meridional_kernel(row_ref, out_ref, *, lat_count):
    block, waves = out_ref.shape
    chunk = 64
    lane = lax.broadcasted_iota(jnp.int32, (1, LANES), 1)
    for start in range(0, block, chunk):
        row = row_ref[start : start + chunk, :]
        weight = jnp.where(row < 0, 0.0, math.sqrt(2.0 / lat_count)).astype(F32)
        rate = (2 * row + 1).astype(F32)
        tiles = cosine_rows(rate, 0.0, 4.0 * lat_count, weight, waves // LANES)
        for index, tile in enumerate(tiles):
            if index == 0:
                tile = jnp.where(lane == 0, tile * math.sqrt(0.5), tile)
            out_ref[start : start + chunk, index * LANES : (index + 1) * LANES] = tile.astype(BF16)


def spectral_kernel(cut_ref, waves_ref, far_ref, own_ref, out_ref, power_ref, table_ref, arrived, *, slots):
    chunks = arrived.shape[0]
    size = table_ref.shape[0] // chunks
    copies = []
    for chunk in range(chunks):
        part = pl.ds(chunk * size, size)
        copies.append(pltpu.make_async_copy(far_ref.at[part], table_ref.at[part], arrived.at[chunk]))
        copies[-1].start()
    spectra = None
    for chunk in range(chunks):
        copies[chunk].wait()
        part = pl.ds(chunk * size, size)
        term = lax.dot_general(
            waves_ref[part], table_ref[part], (((0,), (0,)), ((), ())), preferred_element_type=F32
        )
        spectra = term if spectra is None else spectra + term
    table = table_ref[...]
    fields = 2 * slots
    count = 2 * fields
    spectra = spectra[0:count, :].astype(BF16)
    wide = spectra.astype(F32)
    square = wide * wide
    for level in range(2):
        base = level * fields
        power_ref[level] = square[base : base + slots, :] + square[base + slots : base + fields, :]
    wave = own_ref[...]
    degree = lax.broadcasted_iota(jnp.int32, wide.shape, 1)
    kappa = degree * degree + wave * wave
    below = [kappa < cut_ref[i] * cut_ref[i] for i in range(SENT_BANDS)]
    parts = []
    for band in range(SENT_BANDS):
        keep = below[band]
        if band:
            keep = jnp.logical_and(keep, jnp.logical_not(below[band - 1]))
        parts.append(jnp.where(keep, wide, 0.0).astype(BF16))
    masked = jnp.concatenate(parts, axis=0)
    band_waves = lax.dot_general(masked, table, (((1,), (1,)), ((), ())), preferred_element_type=F32)
    rows = 20
    for dest in range(out_ref.shape[0]):
        pieces = []
        for piece in range(2 * SENT_BANDS):
            part = band_waves[piece * fields : (piece + 1) * fields, :]
            pieces.append(move_lanes(part, dest * ROW_PAD, piece * rows))
        out_ref[dest] = join_lanes(pieces, rows).astype(BF16)


def inverse_kernel(spans, first, *refs):
    if first:
        place_ref, waves_ref, odd_ref, x_ref, far_ref, keep_ref, send_ref, lhs, field, table, arrived = refs
        levels, rows, lon_count = x_ref.shape
    else:
        place_ref, lhs, field, far_ref, keep_ref, send_ref, table, arrived = refs
        lon_count = field.shape[1]
    half = lon_count // 2
    kept = field.shape[0]
    width = keep_ref.shape[2]
    copies = []
    for index, (start, _) in enumerate(spans):
        part = far_ref.at[:, pl.ds(start, width)]
        copies.append(pltpu.make_async_copy(part, table.at[index], arrived.at[index]))
        copies[-1].start()
    if first:
        waves = jnp.transpose(waves_ref[...].astype(F32))
        flag = odd_ref[0:1, :] == 1
        lhs[0:LANES, :] = jnp.where(flag, 0.0, waves).astype(BF16)
        lhs[LANES:, :] = jnp.where(flag, waves, 0.0).astype(BF16)
        for level in range(levels):
            field[level * rows : (level + 1) * rows, :] = x_ref[level].astype(F32)
        values = field[...]
        lane = lax.broadcasted_iota(jnp.int32, values.shape, 1)
        sign = 1.0 - 2.0 * (lane % 2).astype(F32)
        mean = jnp.sum(values * sign, axis=1, keepdims=True) * (1.0 / lon_count)
        field[...] = values - mean * sign

    core = place_ref[0]
    for index, (start, owner) in enumerate(spans):
        copies[index].wait()
        both = jnp.dot(lhs[...], table[index], preferred_element_type=F32)
        even, odd = both[:LANES], both[LANES:]
        for side in range(2):
            bands = even + odd if side == 0 else even - odd
            bands = bands.astype(BF16).astype(F32)
            base = start + side * half
            rest = field[:, base : base + width]
            for band in range(SENT_BANDS):
                rest = rest - bands[band * kept : (band + 1) * kept]
            full = jnp.concatenate([bands[: SENT_BANDS * kept], rest], axis=0).astype(BF16)

            @pl.when(core == owner)
            def _(full=full, side=side):
                keep_ref[side] = full

            @pl.when(core != owner)
            def _(full=full, side=side):
                send_ref[side] = full


def terms_of(first, second, rows, bands):
    a, b = first.astype(F32), second.astype(F32)
    cross = []
    for band in range(bands):
        low = band * 2 * rows
        mid, high = low + rows, low + 2 * rows
        cross.append(a[low:mid] * a[mid:high] + b[low:mid] * b[mid:high])
    return [a * a + b * b] + cross


def pair_kernel(place_ref, keep_ref, came_ref, *refs, rows, bands):
    power_ref = refs[0] if len(refs) == 3 else None
    own_ref, send_ref = refs[-2:]
    side = place_ref[1]

    def put(which, out_ref):
        pieces = terms_of(keep_ref[which], came_ref[which], rows, bands)
        if power_ref is not None:
            pieces.append(power_ref[which])
        out_ref[...] = jnp.concatenate(pieces, axis=0).astype(out_ref.dtype)

    put(1 - side, send_ref)
    put(side, own_ref)


def final_kernel(*refs, rows, bands, scale, power_scale):
    pairs, (out_ref, power_ref) = refs[:-2], refs[-2:]
    wide = 2 * rows * bands
    start = 0
    for index in range(0, len(pairs), 2):
        total = pairs[index][...] + pairs[index + 1][...].astype(F32)
        stop = start + total.shape[1]
        stats = total[: 3 * rows * bands] * scale
        for band in range(bands):
            low = band * 2 * rows
            out_ref[0, :, band, start:stop] = stats[low : low + rows]
            out_ref[1, :, band, start:stop] = stats[low + rows : low + 2 * rows]
            out_ref[2, :, band, start:stop] = stats[wide + band * rows : wide + (band + 1) * rows]
        if index == 0:
            count = power_ref.shape[2]
            power = total[3 * rows * bands :, :count] * power_scale
            slots = power_ref.shape[0]
            for level in range(power_ref.shape[1]):
                power_ref[:, level, :] = power[level * slots : (level + 1) * slots]
        start = stop


VMEM_LIMIT = 24 * 1024 * 1024
WIDE_LIMIT = 52_000_000
WIDER_LIMIT = 54_000_000
WHOLE = pl.BlockSpec(memory_space=pltpu.VMEM)
FAR = pl.BlockSpec(memory_space=pltpu.HBM)
SCALARS = pl.BlockSpec(memory_space=pltpu.SMEM)


def params(limit=VMEM_LIMIT):
    return pltpu.CompilerParams(vmem_limit_bytes=limit)


def shards(perturbations, row_map, wave_map, cutoffs):
    _, levels, rows, lon_count = perturbations.shape
    lat_dev = lax.axis_size("lat")
    mem_dev = lax.axis_size("mem")
    lat = lax.axis_index("lat")
    mem = lax.axis_index("mem")
    swap = lambda value, bit: lax.ppermute(value, "mem", [(i, i ^ bit) for i in range(mem_dev)])
    lat_count = rows * lat_dev
    slot_count = wave_map.shape[0]
    slots = slot_count // lat_dev
    degrees = row_map.shape[0]
    bands = cutoffs.shape[0] + 1
    half = lon_count // 2
    x = perturbations[0]

    columns = 2 * slot_count
    block = 320
    table, outgoing, odd = pl.pallas_call(
        functools.partial(forward_kernel, slots=slots),
        grid=(columns // (2 * block),),
        in_specs=[
            pl.BlockSpec((levels, rows, lon_count), lambda i: (0, 0, 0)),
            pl.BlockSpec((1, slot_count), lambda i: (0, 0)),
        ],
        out_specs=[
            pl.BlockSpec((2 * block, half), lambda i: (i, 0)),
            pl.BlockSpec((lat_dev, ROW_PAD, LANES), lambda i: (0, 0, 0)),
            pl.BlockSpec((8, columns), lambda i: (0, 0)),
        ],
        out_shape=[
            pltpu.HBM((columns, half), BF16),
            jax.ShapeDtypeStruct((lat_dev, ROW_PAD, LANES), BF16),
            jax.ShapeDtypeStruct((8, columns), jnp.int32),
        ],
        scratch_shapes=[
            pltpu.VMEM((LANES, half), BF16),
            pltpu.VMEM((columns // block, LANES, 384), F32),
            pltpu.VMEM((columns, 8), F32),
            pltpu.VMEM((block, half), BF16),
        ],
        compiler_params=params(),
        cost_estimate=pl.CostEstimate(flops=10**9, bytes_accessed=7 * 10**6, transcendentals=0),
        name="forward_zonal",
    )(x, wave_map.reshape(1, slot_count))

    incoming = lax.all_to_all(outgoing, "lat", 0, 0, tiled=True).reshape(lat_dev * ROW_PAD, LANES)

    row_code = jnp.pad(
        row_map.reshape(lat_dev, rows), ((0, 0), (0, ROW_PAD - rows)), constant_values=-1
    ).reshape(lat_dev * ROW_PAD, 1)
    lat_block = 512
    meridional = pl.pallas_call(
        functools.partial(meridional_kernel, lat_count=lat_count),
        grid=(lat_dev * ROW_PAD // lat_block,),
        in_specs=[pl.BlockSpec((lat_block, 1), lambda i: (i, 0))],
        out_specs=pl.BlockSpec((lat_block, degrees), lambda i: (i, 0)),
        out_shape=pltpu.HBM((lat_dev * ROW_PAD, degrees), BF16),
        compiler_params=params(),
        cost_estimate=pl.CostEstimate(flops=10**9, bytes_accessed=4 * 10**6, transcendentals=0),
        name="meridional_table",
    )(row_code)

    own = lax.dynamic_slice_in_dim(wave_map, lat * slots, slots)
    own_rows = jnp.tile(own, 4).reshape(4 * slots, 1)
    band_out, power_terms = pl.pallas_call(
        functools.partial(spectral_kernel, slots=slots),
        in_specs=[SCALARS, WHOLE, FAR, WHOLE],
        out_specs=[WHOLE, WHOLE],
        out_shape=[
            jax.ShapeDtypeStruct((lat_dev, 2 * slots, LANES), BF16),
            jax.ShapeDtypeStruct((levels, slots, degrees), F32),
        ],
        scratch_shapes=[pltpu.VMEM(meridional.shape, BF16), pltpu.SemaphoreType.DMA((6,))],
        compiler_params=params(WIDER_LIMIT),
        cost_estimate=pl.CostEstimate(flops=15 * 10**8, bytes_accessed=6 * 10**6, transcendentals=0),
        name="spectral_bands",
    )(cutoffs, incoming, meridional, own_rows)

    returned = lax.all_to_all(band_out, "lat", 0, 0, tiled=True).reshape(columns, LANES)
    core, side = mem % 2, mem // 2
    place = jnp.stack([core, side]).astype(jnp.int32)
    lon_dev = lon_count // mem_dev
    widths = (384, lon_dev - 384)
    share = degrees // mem_dev
    parts = power_terms.reshape(levels, slots, 2, 2, share).transpose(3, 2, 0, 1, 4)
    other = lax.dynamic_index_in_dim(parts, 1 - core, 0, keepdims=False).astype(BF16)
    power = lax.dynamic_index_in_dim(parts, core, 0, keepdims=False) + swap(other, 1).astype(F32)
    power = jnp.pad(
        power.reshape(2, levels * slots, share), ((0, 0), (0, 0), (0, widths[0] - share))
    )

    kept = levels * rows * bands
    term_rows = 3 * rows * bands
    prepared = None
    ready = []
    start = 0
    for index, width in enumerate(widths):
        spans = [(start, 0), (start + lon_dev, 1)]
        start += width
        first = index == 0
        pair_shape = jax.ShapeDtypeStruct((2, kept, width), BF16)
        out_shape = [pair_shape, pair_shape]
        if first:
            operands = (place, returned, odd, x, table)
            out_shape += [
                jax.ShapeDtypeStruct((2 * LANES, columns), BF16),
                jax.ShapeDtypeStruct((levels * rows, lon_count), F32),
            ]
        else:
            operands = (place, *prepared, table)
        keep, send, *made = pl.pallas_call(
            functools.partial(inverse_kernel, spans, first),
            in_specs=[SCALARS] + [WHOLE] * (len(operands) - 2) + [FAR],
            out_specs=[WHOLE] * len(out_shape),
            out_shape=out_shape,
            scratch_shapes=[
                pltpu.VMEM((len(spans), columns, width), BF16),
                pltpu.SemaphoreType.DMA((len(spans),)),
            ],
            compiler_params=params(WIDE_LIMIT),
            cost_estimate=pl.CostEstimate(flops=10**9, bytes_accessed=4 * 10**6, transcendentals=0),
            name="inverse_zonal",
        )(*operands)
        prepared = made or prepared
        ready.append((keep, swap(send, 1)))
    sums = []
    for index, (keep, came) in enumerate(ready):
        extra = [power] if index == 0 else []
        total_rows = term_rows + (levels * slots if extra else 0)
        own_terms, send_terms = pl.pallas_call(
            functools.partial(pair_kernel, rows=rows, bands=bands),
            in_specs=[SCALARS] + [WHOLE] * (2 + len(extra)),
            out_specs=[WHOLE, WHOLE],
            out_shape=[
                jax.ShapeDtypeStruct((total_rows, widths[index]), F32),
                jax.ShapeDtypeStruct((total_rows, widths[index]), BF16),
            ],
            compiler_params=params(),
            name="pair_terms",
        )(place, keep, came, *extra)
        sums += [own_terms, swap(send_terms, 2)]
    band_stats, power = pl.pallas_call(
        functools.partial(
            final_kernel,
            rows=rows,
            bands=bands,
            scale=1.0 / (mem_dev - 1),
            power_scale=0.5 / (mem_dev - 1),
        ),
        in_specs=[WHOLE] * len(sums),
        out_specs=[WHOLE, WHOLE],
        out_shape=[
            jax.ShapeDtypeStruct((3, rows, bands, lon_dev), F32),
            jax.ShapeDtypeStruct((slots, levels, share), F32),
        ],
        compiler_params=params(),
        name="final_terms",
    )(*sums)
    return (band_stats.transpose(2, 0, 1, 3), power.transpose(1, 2, 0))


def solution(mesh):
    placed = (P("mem", None, "lat", None), P(), P(), P())
    return jax.shard_map(
        shards,
        mesh=mesh,
        in_specs=placed,
        out_specs=(P(None, None, "lat", "mem"), P(None, "mem", "lat")),
        check_vma=False,
    )
```

```python
import functools
import math

import jax
import jax.numpy as jnp
from jax import lax
from jax.experimental import pallas as pl
from jax.experimental.pallas import tpu as pltpu
from jax.sharding import PartitionSpec as P

F32 = jnp.float32
BF16 = jnp.bfloat16
LANES = 128
ROW_PAD = 24
ROW_HEAD = 16
SENT_BANDS = 3
SINE = (
    6.283185307072579,
    -41.341702116996316,
    81.60522620630826,
    -76.70428132156577,
    42.00980565792769,
    -14.394135376685622,
)


def cos_turn(index, period):
    left = index - jnp.round(index * (1.0 / period)) * period
    quarter = 0.25 - jnp.abs(left * (1.0 / period))
    square = quarter * quarter
    total = jnp.full_like(square, SINE[-1])
    for coefficient in SINE[-2::-1]:
        total = total * square + coefficient
    return total * quarter


def cosine_rows(rate, offset, period, weight, steps):
    lane = lax.broadcasted_iota(jnp.int32, (1, LANES), 1).astype(F32)
    start = rate * lane + offset
    stride = rate * float(LANES)
    before = cos_turn(start, period) * weight
    now = cos_turn(start + stride, period) * weight
    twice = jnp.broadcast_to(2.0 * cos_turn(stride, period), before.shape)
    tiles = [before, now]
    while len(tiles) < steps:
        tiles.append(twice * tiles[-1] - tiles[-2])
    return tiles


def move_lanes(block, source, target):
    tile, inner = divmod(source, LANES)
    first = block[:, tile * LANES : (tile + 1) * LANES]
    if inner + 40 > LANES and (tile + 1) * LANES < block.shape[1]:
        second = block[:, (tile + 1) * LANES : (tile + 2) * LANES]
        lane = lax.broadcasted_iota(jnp.int32, first.shape, 1)
        first = jnp.where(lane >= inner, first, second)
    shift = (target - inner) % LANES
    return pltpu.roll(first, shift, 1) if shift else first


def join_lanes(pieces, width):
    lane = lax.broadcasted_iota(jnp.int32, pieces[0].shape, 1)
    out = jnp.zeros_like(pieces[0])
    for index in range(len(pieces) - 1, -1, -1):
        out = jnp.where(lane < (index + 1) * width, pieces[index], out)
    return out


def swap_parts(block, slots):
    rows, lanes = block.shape
    split = block.reshape(rows // (2 * slots), 2 * slots, lanes)
    return pltpu.roll(split, slots, 1).reshape(rows, lanes)


def wave_rows(wave_ref, slots, rows):
    wave = jnp.broadcast_to(wave_ref[...], (rows, wave_ref.shape[1]))
    count = wave.shape[1]
    lane = lax.broadcasted_iota(jnp.int32, (rows, LANES), 1)
    tiles = []
    for tile in range(2 * count // LANES):
        total = jnp.zeros((rows, LANES), jnp.int32)
        first = tile * LANES // slots
        last = ((tile + 1) * LANES - 1) // slots
        for piece in range(first, last + 1):
            device, part = divmod(piece, 2)
            target = piece * slots - tile * LANES
            moved = move_lanes(wave, device * slots, target % LANES)
            mask = jnp.logical_and(lane >= target, lane < target + slots)
            total = jnp.where(mask, moved + 2048 * part, total)
        tiles.append(total)
    return jnp.concatenate(tiles, axis=1)


def forward_kernel(
    x_ref, wave_ref, far_ref, out_ref, odd_ref, folded, sides, table_ref, left, *, slots, block
):
    levels, rows, lon_count = x_ref.shape
    half = lon_count // 2
    columns = table_ref.shape[1]
    period = float(lon_count)

    code = wave_rows(wave_ref, slots, 8)
    part = lax.shift_right_logical(code, 11)
    wave = code - part * 2048
    flags = wave % 2
    odd_ref[...] = flags
    waved = wave.astype(F32)
    phase = part.astype(F32)
    weight = jnp.where(wave == 0, math.sqrt(1.0 / lon_count), math.sqrt(2.0 / lon_count)).astype(F32)
    turn = waved * float(LANES)
    cosine = cos_turn(turn, period)
    sine = cos_turn(turn - 0.25 * period, period) * (2.0 * phase - 1.0)
    index = lax.broadcasted_iota(jnp.int32, code.shape, 0)
    stack = jnp.where(index == 0, waved, -0.25 * period * phase)
    stack = jnp.where(index == 2, weight, stack)
    stack = jnp.where(index == 3, cosine, stack)
    stack = jnp.where(index == 4, sine, stack)
    sides[...] = jnp.transpose(stack)
    folded[...] = jnp.zeros_like(folded)
    for level in range(levels):
        near = x_ref[level, :, :half].astype(F32)
        far = x_ref[level, :, half:].astype(F32)
        folded[32 * level : 32 * level + rows, :] = (near + far).astype(BF16)
        folded[64 + 32 * level : 64 + 32 * level + rows, :] = (near - far).astype(BF16)

    lane = lax.broadcasted_iota(jnp.int32, (1, LANES), 1).astype(F32)
    chunk = 4 * slots

    def make(base, count):
        for start in range(base, base + count, chunk):
            side = sides[start : start + chunk, :]
            now = cos_turn(side[:, 0:1] * lane + side[:, 1:2], period) * side[:, 2:3]
            cosine = jnp.broadcast_to(side[:, 3:4], now.shape)
            later = now * cosine + swap_parts(now, slots) * side[:, 4:5]
            twice = cosine + cosine
            for index in range(half // LANES):
                table_ref[index, start : start + chunk, :] = now.astype(BF16)
                now, later = later, twice * later - now

    width = 2 * slots

    def multiply(base):
        part = jnp.concatenate([table_ref[i, base : base + block, :] for i in range(half // LANES)], axis=1)
        total = lax.dot_general(folded[...], part, (((1,), (1,)), ((), ())), preferred_element_type=F32)
        odd = flags[0:1, base : base + block] == 1
        parts = []
        for level in range(levels):
            low = 32 * level
            parts.append(jnp.where(odd, total[64 + low : 64 + low + 24], total[low : low + 24]))
        rest = parts[0][16:24] + pltpu.roll(parts[1][16:24], 4, 0)
        parts = [part[0:16] for part in parts]
        for dest in range(block // width):
            pieces = [move_lanes(part, dest * width, i * width) for i, part in enumerate(parts)]
            tile = join_lanes(pieces, width)
            last = move_lanes(rest, dest * width, 2 * width)
            where = lax.broadcasted_iota(jnp.int32, last.shape, 1)
            last = jnp.where(jnp.logical_and(where >= 2 * width, where < 3 * width), last, tile[0:8])
            out_ref[base // width + dest] = jnp.concatenate([last, tile[8:16]], axis=0).astype(BF16)

    copies = []
    for base in range(0, columns, block):
        share = columns // left.shape[0]
        for start in range(base, base + block, share):
            make(start, share)
            part = (slice(None), pl.ds(start, share))
            copies.append(pltpu.make_async_copy(table_ref.at[part], far_ref.at[part], left.at[len(copies)]))
            copies[-1].start()
        if base:
            multiply(base - block)
    multiply(columns - block)
    for copy in copies:
        copy.wait()


def prepare_kernel(
    cut_ref, row_ref, own_ref, far_ref, band_ref, table_ref, left, *, lat_count
):
    total, waves = table_ref.shape
    chunk = 64
    lane = lax.broadcasted_iota(jnp.int32, (1, LANES), 1)

    def make(index, carry):
        rows = pl.ds(pl.multiple_of(index * chunk, chunk), chunk)
        row = row_ref[rows, :]
        weight = jnp.where(row < 0, 0.0, math.sqrt(2.0 / lat_count)).astype(F32)
        rate = (2 * row + 1).astype(F32)
        tiles = cosine_rows(rate, 0.0, 4.0 * lat_count, weight, waves // LANES)
        for place, tile in enumerate(tiles):
            if place == 0:
                tile = jnp.where(lane == 0, tile * math.sqrt(0.5), tile)
            table_ref[rows, place * LANES : (place + 1) * LANES] = tile.astype(BF16)
        return carry

    count = left.shape[0]
    size = total // count
    copies = []
    for piece in range(count):
        lax.fori_loop(piece * size // chunk, (piece + 1) * size // chunk, make, 0)
        part = pl.ds(piece * size, size)
        copies.append(pltpu.make_async_copy(table_ref.at[part], far_ref.at[part], left.at[piece]))
        copies[-1].start()
    wave = own_ref[...]
    count = wave.shape[0]
    degree = lax.broadcasted_iota(jnp.int32, (count, waves), 1)
    kappa = degree * degree + wave * wave
    index = jnp.zeros(kappa.shape, F32)
    for i in range(SENT_BANDS):
        index = index + (kappa >= cut_ref[i] * cut_ref[i]).astype(F32)
    band_ref[...] = index.astype(BF16)
    for copy in copies:
        copy.wait()


def spectral_kernel(
    waves_ref, far_ref, band_ref, out_ref, power_ref, table_ref, arrived, *, slots
):
    chunks = arrived.shape[0]
    size = table_ref.shape[0] // chunks
    copies = []
    for chunk in range(chunks):
        part = pl.ds(chunk * size, size)
        copies.append(pltpu.make_async_copy(far_ref.at[part], table_ref.at[part], arrived.at[chunk]))
        copies[-1].start()
    came = waves_ref[...].astype(F32)
    devices = came.shape[0]
    fields = 2 * slots
    count = 2 * fields
    rest = came[:, 0:8, :].reshape(devices * 8, LANES)
    low = pltpu.roll(rest, LANES - count, 1)
    high = pltpu.roll(pltpu.roll(rest, LANES - count + fields, 1).reshape(devices, 8, LANES), 4, 1)
    lane = lax.broadcasted_iota(jnp.int32, high.shape, 2)
    row = lax.broadcasted_iota(jnp.int32, high.shape, 1)
    rest = jnp.where(lane < fields, low.reshape(high.shape), high)
    rest = jnp.where(row < 4, rest, 0.0)
    waves = jnp.concatenate([came, rest], axis=1).reshape(devices * ROW_PAD, LANES).astype(BF16)
    spectra = None
    for chunk in range(chunks):
        copies[chunk].wait()
        term = lax.dot_general(
            waves[chunk * size : (chunk + 1) * size],
            table_ref[pl.ds(chunk * size, size)],
            (((0,), (0,)), ((), ())),
            preferred_element_type=F32,
        )
        spectra = term if spectra is None else spectra + term
    spectra = spectra[0:count, :].astype(BF16)
    wide = spectra.astype(F32)
    square = wide * wide
    for level in range(2):
        base = level * fields
        power_ref[level] = square[base : base + slots, :] + square[base + slots : base + fields, :]
    index = band_ref[...].astype(F32)
    masked = jnp.concatenate(
        [jnp.where(index == float(band), wide, 0.0).astype(BF16) for band in range(SENT_BANDS)], axis=0
    )
    rows = 20
    groups = 4
    share = devices // groups
    wide_rows = share * ROW_PAD
    for group in range(groups):
        band_waves = lax.dot_general(
            masked,
            table_ref[pl.ds(group * wide_rows, wide_rows)],
            (((1,), (1,)), ((), ())),
            preferred_element_type=F32,
        )
        for dest in range(share):
            pieces = []
            for piece in range(2 * SENT_BANDS):
                part = band_waves[piece * fields : (piece + 1) * fields, :]
                pieces.append(move_lanes(part, dest * ROW_PAD, piece * rows))
            out_ref[group * share + dest] = join_lanes(pieces, rows).astype(BF16)


def fetch_kernel(place_ref, x_ref, far_ref, out_ref, field_ref, arrived, *, width):
    first = (1 - place_ref[0]) * (width // LANES)
    copies = []
    for tile in range(out_ref.shape[0]):
        copies.append(pltpu.make_async_copy(far_ref.at[first + tile], out_ref.at[tile], arrived.at[tile]))
        copies[-1].start()
    levels, rows, lon_count = x_ref.shape
    for level in range(levels):
        field_ref[level * rows : (level + 1) * rows, :] = x_ref[level].astype(F32)
    values = field_ref[...]
    lane = lax.broadcasted_iota(jnp.int32, values.shape, 1)
    sign = 1.0 - 2.0 * (lane % 2).astype(F32)
    mean = jnp.sum(values * sign, axis=1, keepdims=True) * (1.0 / lon_count)
    field_ref[...] = values - mean * sign
    for copy in copies:
        copy.wait()


def beside(ref, start, stop):
    return jnp.concatenate([ref[tile] for tile in range(start, stop)], axis=1)


def put_fields(both, field_ref, out_ref, base, start):
    kept, lon_count = field_ref.shape
    width = both.shape[1]
    even, odd = both[:LANES], both[LANES:]
    for side in range(2):
        bands = even + odd if side == 0 else even - odd
        bands = bands.astype(BF16).astype(F32)
        first = pl.multiple_of(base + start + side * (lon_count // 2), LANES)
        rest = field_ref[:, pl.ds(first, width)]
        for band in range(SENT_BANDS):
            rest = rest - bands[band * kept : (band + 1) * kept]
        full = jnp.concatenate([bands[: SENT_BANDS * kept], rest], axis=0).astype(BF16)
        out_ref[side, :, start : start + width] = full


def inverse_send_kernel(
    place_ref, waves_ref, odd_ref, field_ref, near_ref, far_ref, out_ref, lhs, next_ref, last, arrived
):
    width = out_ref.shape[2]
    core = place_ref[0]
    base = pl.multiple_of((1 - core) * width, LANES)
    tiles = width // LANES
    near = near_ref.shape[0]
    ends = []
    for tile in range(near, tiles):
        source = far_ref.at[(1 - core) * tiles + tile]
        ends.append(pltpu.make_async_copy(source, last.at[tile - near], arrived.at[len(ends)]))
    for tile in range(tiles):
        source = far_ref.at[core * tiles + tile]
        ends.append(pltpu.make_async_copy(source, next_ref.at[tile], arrived.at[len(ends)]))
    for copy in ends:
        copy.start()
    waves = jnp.transpose(waves_ref[...])
    flag = odd_ref[0:1, :] == 1
    zero = jnp.zeros((), BF16)
    lhs[0:LANES, :] = jnp.where(flag, zero, waves)
    lhs[LANES:, :] = jnp.where(flag, waves, zero)
    both = jnp.dot(lhs[...], beside(near_ref, 0, near), preferred_element_type=F32)
    put_fields(both, field_ref, out_ref, base, 0)
    for copy in ends[: tiles - near]:
        copy.wait()
    both = jnp.dot(lhs[...], beside(last, 0, tiles - near), preferred_element_type=F32)
    put_fields(both, field_ref, out_ref, base, near * LANES)
    for copy in ends[tiles - near :]:
        copy.wait()


def inverse_keep_kernel(place_ref, lhs, field_ref, table_ref, out_ref):
    width = out_ref.shape[2]
    base = pl.multiple_of(place_ref[0] * width, LANES)
    for start in range(0, width, 256):
        stop = min(start + 256, width)
        part = beside(table_ref, start // LANES, stop // LANES)
        both = jnp.dot(lhs[...], part, preferred_element_type=F32)
        put_fields(both, field_ref, out_ref, base, start)


def terms_of(first, second, rows, bands):
    a, b = first.astype(F32), second.astype(F32)
    cross = []
    for band in range(bands):
        low = band * 2 * rows
        mid, high = low + rows, low + 2 * rows
        cross.append(a[low:mid] * a[mid:high] + b[low:mid] * b[mid:high])
    return [a * a + b * b] + cross


def pair_kernel(place_ref, keep_ref, came_ref, power_ref, out_ref, *, rows, bands, other):
    which = 1 - place_ref[1] if other else place_ref[1]
    pieces = terms_of(keep_ref[which], came_ref[which], rows, bands)
    pieces.append(power_ref[which])
    out_ref[...] = jnp.concatenate(pieces, axis=0).astype(out_ref.dtype)


def final_kernel(own_ref, came_ref, out_ref, power_ref, *, rows, bands, scale, power_scale):
    wide = 2 * rows * bands
    total = own_ref[...] + came_ref[...].astype(F32)
    stats = total[: 3 * rows * bands] * scale
    for band in range(bands):
        low = band * 2 * rows
        out_ref[0, :, band, :] = stats[low : low + rows]
        out_ref[1, :, band, :] = stats[low + rows : low + 2 * rows]
        out_ref[2, :, band, :] = stats[wide + band * rows : wide + (band + 1) * rows]
    power = total[3 * rows * bands :] * power_scale
    slots, levels, count = power_ref.shape
    for level in range(levels):
        power_ref[:, level, :] = power[:slots, level * count : (level + 1) * count]


VMEM_LIMIT = 24 * 1024 * 1024
WIDE_LIMIT = 44_000_000
FETCH_LIMIT = 54_000_000
WIDER_LIMIT = 54_000_000
WHOLE = pl.BlockSpec(memory_space=pltpu.VMEM)
FAR = pl.BlockSpec(memory_space=pltpu.HBM)
SCALARS = pl.BlockSpec(memory_space=pltpu.SMEM)


def params(limit=VMEM_LIMIT):
    return pltpu.CompilerParams(vmem_limit_bytes=limit)


def shards(perturbations, row_map, wave_map, cutoffs):
    _, levels, rows, lon_count = perturbations.shape
    lat_dev = lax.axis_size("lat")
    mem_dev = lax.axis_size("mem")
    lat = lax.axis_index("lat")
    mem = lax.axis_index("mem")
    swap = lambda value, bit: lax.ppermute(value, "mem", [(i, i ^ bit) for i in range(mem_dev)])
    lat_count = rows * lat_dev
    slot_count = wave_map.shape[0]
    slots = slot_count // lat_dev
    degrees = row_map.shape[0]
    bands = cutoffs.shape[0] + 1
    half = lon_count // 2
    x = perturbations[0]

    columns = 2 * slot_count
    block = 640
    table, outgoing, odd = pl.pallas_call(
        functools.partial(forward_kernel, slots=slots, block=block),
        in_specs=[WHOLE, WHOLE],
        out_specs=[FAR, WHOLE, WHOLE],
        out_shape=[
            pltpu.HBM((half // LANES, columns, LANES), BF16),
            jax.ShapeDtypeStruct((lat_dev, ROW_HEAD, LANES), BF16),
            jax.ShapeDtypeStruct((8, columns), jnp.int32),
        ],
        scratch_shapes=[
            pltpu.VMEM((LANES, half), BF16),
            pltpu.VMEM((columns, 8), F32),
            pltpu.VMEM((half // LANES, columns, LANES), BF16),
            pltpu.SemaphoreType.DMA((16,)),
        ],
        compiler_params=params(),
        cost_estimate=pl.CostEstimate(flops=10**9, bytes_accessed=7 * 10**6, transcendentals=0),
        name="forward_zonal",
    )(x, wave_map.reshape(1, slot_count))

    incoming = lax.all_to_all(outgoing, "lat", 0, 0, tiled=True)

    row_code = jnp.pad(
        row_map.reshape(lat_dev, rows), ((0, 0), (0, ROW_PAD - rows)), constant_values=-1
    ).reshape(lat_dev * ROW_PAD, 1)
    own = lax.dynamic_slice_in_dim(wave_map, lat * slots, slots)
    own_rows = jnp.tile(own, 4).reshape(4 * slots, 1)
    far_table, band_index = pl.pallas_call(
        functools.partial(prepare_kernel, lat_count=lat_count),
        in_specs=[SCALARS, WHOLE, WHOLE],
        out_specs=[FAR, WHOLE],
        out_shape=[
            pltpu.HBM((lat_dev * ROW_PAD, degrees), BF16),
            jax.ShapeDtypeStruct((4 * slots, degrees), BF16),
        ],
        scratch_shapes=[
            pltpu.VMEM((lat_dev * ROW_PAD, degrees), BF16),
            pltpu.SemaphoreType.DMA((6,)),
        ],
        compiler_params=params(),
        cost_estimate=pl.CostEstimate(flops=10**9, bytes_accessed=4 * 10**6, transcendentals=0),
        name="meridional_table",
    )(cutoffs, row_code, own_rows)

    band_out, power_terms = pl.pallas_call(
        functools.partial(spectral_kernel, slots=slots),
        in_specs=[WHOLE, FAR, WHOLE],
        out_specs=[WHOLE, WHOLE],
        out_shape=[
            jax.ShapeDtypeStruct((lat_dev, 2 * slots, LANES), BF16),
            jax.ShapeDtypeStruct((levels, slots, degrees), F32),
        ],
        scratch_shapes=[pltpu.VMEM(far_table.shape, BF16), pltpu.SemaphoreType.DMA((6,))],
        compiler_params=params(WIDER_LIMIT),
        cost_estimate=pl.CostEstimate(flops=15 * 10**8, bytes_accessed=6 * 10**6, transcendentals=0),
        name="spectral_bands",
    )(incoming, far_table, band_index)

    returned = lax.all_to_all(band_out, "lat", 0, 0, tiled=True).reshape(columns, LANES)
    core, side = mem % 2, mem // 2
    place = jnp.stack([core, side]).astype(jnp.int32)
    lon_dev = lon_count // mem_dev
    share = degrees // mem_dev
    parts = power_terms.reshape(levels, slots, 2, 2, share).transpose(3, 2, 1, 0, 4)
    other = lax.dynamic_index_in_dim(parts, 1 - core, 0, keepdims=False).astype(BF16)
    power = lax.dynamic_index_in_dim(parts, core, 0, keepdims=False) + swap(other, 1).astype(F32)
    power = jnp.pad(power.reshape(2, slots, levels * share), ((0, 0), (0, ROW_PAD - slots), (0, 0)))

    lon_dev = lon_count // mem_dev
    kept = levels * rows * bands
    term_rows = 3 * rows * bands + ROW_PAD
    pair_shape = jax.ShapeDtypeStruct((2, kept, lon_dev), BF16)
    lhs_shape = jax.ShapeDtypeStruct((2 * LANES, columns), BF16)
    place, power = lax.optimization_barrier((place, power))

    near_tiles = 3
    tiles = lon_dev // LANES
    after, _ = lax.optimization_barrier((place, power_terms))
    near_zonal, field = pl.pallas_call(
        functools.partial(fetch_kernel, width=lon_dev),
        in_specs=[SCALARS, WHOLE, FAR],
        out_specs=[WHOLE, WHOLE],
        out_shape=[
            pltpu.VMEM((near_tiles, columns, LANES), BF16),
            pltpu.VMEM((levels * rows, lon_count), F32),
        ],
        scratch_shapes=[pltpu.SemaphoreType.DMA((near_tiles,))],
        compiler_params=params(FETCH_LIMIT),
        cost_estimate=pl.CostEstimate(flops=10**9, bytes_accessed=5 * 10**6, transcendentals=0),
        name="fetch_table",
    )(after, x, table)
    send, lhs, next_zonal = pl.pallas_call(
        inverse_send_kernel,
        in_specs=[SCALARS, WHOLE, WHOLE, WHOLE, WHOLE, FAR],
        out_specs=[WHOLE, WHOLE, WHOLE],
        out_shape=[pair_shape, lhs_shape, pltpu.VMEM((tiles, columns, LANES), BF16)],
        scratch_shapes=[
            pltpu.VMEM((tiles - near_tiles, columns, LANES), BF16),
            pltpu.SemaphoreType.DMA((2 * tiles - near_tiles,)),
        ],
        compiler_params=params(WIDE_LIMIT),
        cost_estimate=pl.CostEstimate(flops=10**9, bytes_accessed=5 * 10**6, transcendentals=0),
        name="inverse_send",
    )(place, returned, odd, field, near_zonal, table)
    came = swap(send, 1)
    keep = pl.pallas_call(
        inverse_keep_kernel,
        in_specs=[SCALARS] + [WHOLE] * 3,
        out_specs=WHOLE,
        out_shape=pair_shape,
        compiler_params=params(),
        cost_estimate=pl.CostEstimate(flops=10**9, bytes_accessed=5 * 10**6, transcendentals=0),
        name="inverse_keep",
    )(place, lhs, field, next_zonal)

    def pair(other, dtype):
        return pl.pallas_call(
            functools.partial(pair_kernel, rows=rows, bands=bands, other=other),
            in_specs=[SCALARS] + [WHOLE] * 3,
            out_specs=WHOLE,
            out_shape=jax.ShapeDtypeStruct((term_rows, lon_dev), dtype),
            compiler_params=params(),
            name="pair_terms",
        )(place, keep, came, power)

    came_terms = swap(pair(True, BF16), 2)
    band_stats, power = pl.pallas_call(
        functools.partial(
            final_kernel,
            rows=rows,
            bands=bands,
            scale=1.0 / (mem_dev - 1),
            power_scale=0.5 / (mem_dev - 1),
        ),
        in_specs=[WHOLE, WHOLE],
        out_specs=[WHOLE, WHOLE],
        out_shape=[
            jax.ShapeDtypeStruct((3, rows, bands, lon_dev), F32),
            jax.ShapeDtypeStruct((slots, levels, share), F32),
        ],
        compiler_params=params(),
        name="final_terms",
    )(pair(False, F32), came_terms)
    return (band_stats.transpose(2, 0, 1, 3), power.transpose(1, 2, 0))


def solution(mesh):
    placed = (P("mem", None, "lat", None), P(), P(), P())
    return jax.shard_map(
        shards,
        mesh=mesh,
        in_specs=placed,
        out_specs=(P(None, None, "lat", "mem"), P(None, "mem", "lat")),
        check_vma=False,
    )
```

```python
import functools
import math

import jax
import jax.numpy as jnp
from jax import lax
from jax.experimental import pallas as pl
from jax.experimental.pallas import tpu as pltpu
from jax.sharding import PartitionSpec as P

F32 = jnp.float32
BF16 = jnp.bfloat16
LANES = 128
ROW_PAD = 24
ROW_HEAD = 16
SENT_BANDS = 3
SINE = (
    6.283185307072579,
    -41.341702116996316,
    81.60522620630826,
    -76.70428132156577,
    42.00980565792769,
    -14.394135376685622,
)


def cos_turn(index, period):
    left = index - jnp.round(index * (1.0 / period)) * period
    quarter = 0.25 - jnp.abs(left * (1.0 / period))
    square = quarter * quarter
    total = jnp.full_like(square, SINE[-1])
    for coefficient in SINE[-2::-1]:
        total = total * square + coefficient
    return total * quarter


def cosine_rows(rate, offset, period, weight, steps):
    lane = lax.broadcasted_iota(jnp.int32, (1, LANES), 1).astype(F32)
    start = rate * lane + offset
    stride = rate * float(LANES)
    before = cos_turn(start, period) * weight
    now = cos_turn(start + stride, period) * weight
    twice = jnp.broadcast_to(2.0 * cos_turn(stride, period), before.shape)
    tiles = [before, now]
    while len(tiles) < steps:
        tiles.append(twice * tiles[-1] - tiles[-2])
    return tiles


def move_lanes(block, source, target):
    tile, inner = divmod(source, LANES)
    first = block[:, tile * LANES : (tile + 1) * LANES]
    if inner + 40 > LANES and (tile + 1) * LANES < block.shape[1]:
        second = block[:, (tile + 1) * LANES : (tile + 2) * LANES]
        lane = lax.broadcasted_iota(jnp.int32, first.shape, 1)
        first = jnp.where(lane >= inner, first, second)
    shift = (target - inner) % LANES
    return pltpu.roll(first, shift, 1) if shift else first


def join_lanes(pieces, width):
    lane = lax.broadcasted_iota(jnp.int32, pieces[0].shape, 1)
    out = jnp.zeros_like(pieces[0])
    for index in range(len(pieces) - 1, -1, -1):
        out = jnp.where(lane < (index + 1) * width, pieces[index], out)
    return out


def swap_parts(block, slots):
    rows, lanes = block.shape
    split = block.reshape(rows // (2 * slots), 2 * slots, lanes)
    return pltpu.roll(split, slots, 1).reshape(rows, lanes)


def wave_rows(wave_ref, slots, rows):
    wave = jnp.broadcast_to(wave_ref[...], (rows, wave_ref.shape[1]))
    count = wave.shape[1]
    lane = lax.broadcasted_iota(jnp.int32, (rows, LANES), 1)
    tiles = []
    for tile in range(2 * count // LANES):
        total = jnp.zeros((rows, LANES), jnp.int32)
        first = tile * LANES // slots
        last = ((tile + 1) * LANES - 1) // slots
        for piece in range(first, last + 1):
            device, part = divmod(piece, 2)
            target = piece * slots - tile * LANES
            moved = move_lanes(wave, device * slots, target % LANES)
            mask = jnp.logical_and(lane >= target, lane < target + slots)
            total = jnp.where(mask, moved + 2048 * part, total)
        tiles.append(total)
    return jnp.concatenate(tiles, axis=1)


def forward_kernel(
    x_ref, wave_ref, far_ref, out_ref, odd_ref, folded, sides, table_ref, left, *, slots, block
):
    levels, rows, lon_count = x_ref.shape
    half = lon_count // 2
    columns = table_ref.shape[1]
    period = float(lon_count)

    code = wave_rows(wave_ref, slots, 8)
    part = lax.shift_right_logical(code, 11)
    wave = code - part * 2048
    flags = wave % 2
    odd_ref[...] = flags
    waved = wave.astype(F32)
    phase = part.astype(F32)
    weight = jnp.where(wave == 0, math.sqrt(1.0 / lon_count), math.sqrt(2.0 / lon_count)).astype(F32)
    turn = waved * float(LANES)
    cosine = cos_turn(turn, period)
    sine = cos_turn(turn - 0.25 * period, period) * (2.0 * phase - 1.0)
    index = lax.broadcasted_iota(jnp.int32, code.shape, 0)
    stack = jnp.where(index == 0, waved, -0.25 * period * phase)
    stack = jnp.where(index == 2, weight, stack)
    stack = jnp.where(index == 3, cosine, stack)
    stack = jnp.where(index == 4, sine, stack)
    sides[...] = jnp.transpose(stack)
    folded[...] = jnp.zeros_like(folded)
    for level in range(levels):
        near = x_ref[level, :, :half].astype(F32)
        far = x_ref[level, :, half:].astype(F32)
        folded[32 * level : 32 * level + rows, :] = (near + far).astype(BF16)
        folded[64 + 32 * level : 64 + 32 * level + rows, :] = (near - far).astype(BF16)

    lane = lax.broadcasted_iota(jnp.int32, (1, LANES), 1).astype(F32)
    chunk = 4 * slots

    def make(base, count):
        for start in range(base, base + count, chunk):
            side = sides[start : start + chunk, :]
            now = cos_turn(side[:, 0:1] * lane + side[:, 1:2], period) * side[:, 2:3]
            cosine = jnp.broadcast_to(side[:, 3:4], now.shape)
            later = now * cosine + swap_parts(now, slots) * side[:, 4:5]
            twice = cosine + cosine
            for index in range(half // LANES):
                table_ref[index, start : start + chunk, :] = now.astype(BF16)
                now, later = later, twice * later - now

    width = 2 * slots

    def multiply(base):
        part = jnp.concatenate([table_ref[i, base : base + block, :] for i in range(half // LANES)], axis=1)
        total = lax.dot_general(folded[...], part, (((1,), (1,)), ((), ())), preferred_element_type=F32)
        odd = flags[0:1, base : base + block] == 1
        parts = []
        for level in range(levels):
            low = 32 * level
            parts.append(jnp.where(odd, total[64 + low : 64 + low + 24], total[low : low + 24]))
        rest = parts[0][16:24] + pltpu.roll(parts[1][16:24], 4, 0)
        parts = [part[0:16] for part in parts]
        for dest in range(block // width):
            pieces = [move_lanes(part, dest * width, i * width) for i, part in enumerate(parts)]
            tile = join_lanes(pieces, width)
            last = move_lanes(rest, dest * width, 2 * width)
            where = lax.broadcasted_iota(jnp.int32, last.shape, 1)
            last = jnp.where(jnp.logical_and(where >= 2 * width, where < 3 * width), last, tile[0:8])
            out_ref[base // width + dest] = jnp.concatenate([last, tile[8:16]], axis=0).astype(BF16)

    copies = []
    for base in range(0, columns, block):
        share = columns // left.shape[0]
        for start in range(base, base + block, share):
            make(start, share)
            part = (slice(None), pl.ds(start, share))
            copies.append(pltpu.make_async_copy(table_ref.at[part], far_ref.at[part], left.at[len(copies)]))
            copies[-1].start()
        if base:
            multiply(base - block)
    multiply(columns - block)
    for copy in copies:
        copy.wait()


def prepare_kernel(
    cut_ref, row_ref, own_ref, far_ref, band_ref, table_ref, left, *, lat_count
):
    total, waves = table_ref.shape
    chunk = 64
    lane = lax.broadcasted_iota(jnp.int32, (1, LANES), 1)

    def make(index, carry):
        rows = pl.ds(pl.multiple_of(index * chunk, chunk), chunk)
        row = row_ref[rows, :]
        weight = jnp.where(row < 0, 0.0, math.sqrt(2.0 / lat_count)).astype(F32)
        rate = (2 * row + 1).astype(F32)
        tiles = cosine_rows(rate, 0.0, 4.0 * lat_count, weight, waves // LANES)
        for place, tile in enumerate(tiles):
            if place == 0:
                tile = jnp.where(lane == 0, tile * math.sqrt(0.5), tile)
            table_ref[rows, place * LANES : (place + 1) * LANES] = tile.astype(BF16)
        return carry

    count = left.shape[0]
    size = total // count
    copies = []
    for piece in range(count):
        lax.fori_loop(piece * size // chunk, (piece + 1) * size // chunk, make, 0)
        part = pl.ds(piece * size, size)
        copies.append(pltpu.make_async_copy(table_ref.at[part], far_ref.at[part], left.at[piece]))
        copies[-1].start()
    wave = own_ref[...]
    count = wave.shape[0]
    degree = lax.broadcasted_iota(jnp.int32, (count, waves), 1)
    kappa = degree * degree + wave * wave
    index = jnp.zeros(kappa.shape, F32)
    for i in range(SENT_BANDS):
        index = index + (kappa >= cut_ref[i] * cut_ref[i]).astype(F32)
    band_ref[...] = index.astype(BF16)
    for copy in copies:
        copy.wait()


def spectral_kernel(
    waves_ref, far_ref, band_ref, out_ref, power_ref, table_ref, arrived, *, slots
):
    chunks = arrived.shape[0]
    size = table_ref.shape[0] // chunks
    copies = []
    for chunk in range(chunks):
        part = pl.ds(chunk * size, size)
        copies.append(pltpu.make_async_copy(far_ref.at[part], table_ref.at[part], arrived.at[chunk]))
        copies[-1].start()
    came = waves_ref[...].astype(F32)
    devices = came.shape[0]
    fields = 2 * slots
    count = 2 * fields
    rest = came[:, 0:8, :].reshape(devices * 8, LANES)
    low = pltpu.roll(rest, LANES - count, 1)
    high = pltpu.roll(pltpu.roll(rest, LANES - count + fields, 1).reshape(devices, 8, LANES), 4, 1)
    lane = lax.broadcasted_iota(jnp.int32, high.shape, 2)
    row = lax.broadcasted_iota(jnp.int32, high.shape, 1)
    rest = jnp.where(lane < fields, low.reshape(high.shape), high)
    rest = jnp.where(row < 4, rest, 0.0)
    waves = jnp.concatenate([came, rest], axis=1).reshape(devices * ROW_PAD, LANES).astype(BF16)
    spectra = None
    for chunk in range(chunks):
        copies[chunk].wait()
        term = lax.dot_general(
            waves[chunk * size : (chunk + 1) * size],
            table_ref[pl.ds(chunk * size, size)],
            (((0,), (0,)), ((), ())),
            preferred_element_type=F32,
        )
        spectra = term if spectra is None else spectra + term
    spectra = spectra[0:count, :].astype(BF16)
    wide = spectra.astype(F32)
    square = wide * wide
    for level in range(2):
        base = level * fields
        power_ref[level] = square[base : base + slots, :] + square[base + slots : base + fields, :]
    index = band_ref[...].astype(F32)
    masked = jnp.concatenate(
        [jnp.where(index == float(band), wide, 0.0).astype(BF16) for band in range(SENT_BANDS)], axis=0
    )
    rows = 20
    groups = 4
    share = devices // groups
    wide_rows = share * ROW_PAD
    for group in range(groups):
        band_waves = lax.dot_general(
            masked,
            table_ref[pl.ds(group * wide_rows, wide_rows)],
            (((1,), (1,)), ((), ())),
            preferred_element_type=F32,
        )
        for dest in range(share):
            pieces = []
            for piece in range(2 * SENT_BANDS):
                part = band_waves[piece * fields : (piece + 1) * fields, :]
                pieces.append(move_lanes(part, dest * ROW_PAD, piece * rows))
            out_ref[group * share + dest] = join_lanes(pieces, rows).astype(BF16)


def fetch_kernel(place_ref, x_ref, far_ref, out_ref, field_ref, arrived, *, width):
    first = (1 - place_ref[0]) * (width // LANES)
    copies = []
    for tile in range(out_ref.shape[0]):
        copies.append(pltpu.make_async_copy(far_ref.at[first + tile], out_ref.at[tile], arrived.at[tile]))
        copies[-1].start()
    levels, rows, lon_count = x_ref.shape
    for level in range(levels):
        field_ref[level * rows : (level + 1) * rows, :] = x_ref[level].astype(F32)
    values = field_ref[...]
    lane = lax.broadcasted_iota(jnp.int32, values.shape, 1)
    sign = 1.0 - 2.0 * (lane % 2).astype(F32)
    mean = jnp.sum(values * sign, axis=1, keepdims=True) * (1.0 / lon_count)
    field_ref[...] = values - mean * sign
    for copy in copies:
        copy.wait()


def beside(ref, start, stop):
    return jnp.concatenate([ref[tile] for tile in range(start, stop)], axis=1)


def put_fields(both, field_ref, out_ref, base, start):
    kept, lon_count = field_ref.shape
    width = both.shape[1]
    even, odd = both[:LANES], both[LANES:]
    for side in range(2):
        bands = even + odd if side == 0 else even - odd
        bands = bands.astype(BF16).astype(F32)
        first = pl.multiple_of(base + start + side * (lon_count // 2), LANES)
        rest = field_ref[:, pl.ds(first, width)]
        for band in range(SENT_BANDS):
            rest = rest - bands[band * kept : (band + 1) * kept]
        full = jnp.concatenate([bands[: SENT_BANDS * kept], rest], axis=0).astype(BF16)
        out_ref[side, :, start : start + width] = full


def inverse_send_kernel(
    place_ref, waves_ref, odd_ref, field_ref, near_ref, far_ref, out_ref, lhs, next_ref, last, arrived
):
    width = out_ref.shape[2]
    core = place_ref[0]
    base = pl.multiple_of((1 - core) * width, LANES)
    tiles = width // LANES
    near = near_ref.shape[0]
    ends = []
    for tile in range(near, tiles):
        source = far_ref.at[(1 - core) * tiles + tile]
        ends.append(pltpu.make_async_copy(source, last.at[tile - near], arrived.at[len(ends)]))
    for tile in range(tiles):
        source = far_ref.at[core * tiles + tile]
        ends.append(pltpu.make_async_copy(source, next_ref.at[tile], arrived.at[len(ends)]))
    for copy in ends:
        copy.start()
    waves = jnp.transpose(waves_ref[...].astype(F32))
    odd = waves * odd_ref[0:1, :].astype(F32)
    lhs[0:LANES, :] = (waves - odd).astype(BF16)
    lhs[LANES:, :] = odd.astype(BF16)
    both = jnp.dot(lhs[...], beside(near_ref, 0, near), preferred_element_type=F32)
    put_fields(both, field_ref, out_ref, base, 0)
    for copy in ends[: tiles - near]:
        copy.wait()
    both = jnp.dot(lhs[...], beside(last, 0, tiles - near), preferred_element_type=F32)
    put_fields(both, field_ref, out_ref, base, near * LANES)
    for copy in ends[tiles - near :]:
        copy.wait()


def inverse_keep_kernel(place_ref, lhs, field_ref, table_ref, out_ref):
    width = out_ref.shape[2]
    base = pl.multiple_of(place_ref[0] * width, LANES)
    for start in range(0, width, 256):
        stop = min(start + 256, width)
        part = beside(table_ref, start // LANES, stop // LANES)
        both = jnp.dot(lhs[...], part, preferred_element_type=F32)
        put_fields(both, field_ref, out_ref, base, start)


def terms_of(first, second, rows, bands):
    a, b = first.astype(F32), second.astype(F32)
    cross = []
    for band in range(bands):
        low = band * 2 * rows
        mid, high = low + rows, low + 2 * rows
        cross.append(a[low:mid] * a[mid:high] + b[low:mid] * b[mid:high])
    return [a * a + b * b] + cross


def pair_kernel(place_ref, keep_ref, came_ref, out_ref, *, rows, bands, other):
    which = 1 - place_ref[1] if other else place_ref[1]
    pieces = terms_of(keep_ref[which], came_ref[which], rows, bands)
    out_ref[...] = jnp.concatenate(pieces, axis=0).astype(out_ref.dtype)


def final_kernel(own_ref, came_ref, out_ref, *, rows, bands, scale):
    wide = 2 * rows * bands
    total = own_ref[...] + came_ref[...].astype(F32)
    stats = total[: 3 * rows * bands] * scale
    for band in range(bands):
        low = band * 2 * rows
        out_ref[0, :, band, :] = stats[low : low + rows]
        out_ref[1, :, band, :] = stats[low + rows : low + 2 * rows]
        out_ref[2, :, band, :] = stats[wide + band * rows : wide + (band + 1) * rows]


VMEM_LIMIT = 24 * 1024 * 1024
WIDE_LIMIT = 44_000_000
FETCH_LIMIT = 54_000_000
WIDER_LIMIT = 54_000_000
WHOLE = pl.BlockSpec(memory_space=pltpu.VMEM)
FAR = pl.BlockSpec(memory_space=pltpu.HBM)
SCALARS = pl.BlockSpec(memory_space=pltpu.SMEM)


def params(limit=VMEM_LIMIT):
    return pltpu.CompilerParams(vmem_limit_bytes=limit)


def shards(perturbations, row_map, wave_map, cutoffs):
    _, levels, rows, lon_count = perturbations.shape
    lat_dev = lax.axis_size("lat")
    mem_dev = lax.axis_size("mem")
    lat = lax.axis_index("lat")
    mem = lax.axis_index("mem")
    swap = lambda value, bit: lax.ppermute(value, "mem", [(i, i ^ bit) for i in range(mem_dev)])
    lat_count = rows * lat_dev
    slot_count = wave_map.shape[0]
    slots = slot_count // lat_dev
    degrees = row_map.shape[0]
    bands = cutoffs.shape[0] + 1
    half = lon_count // 2
    x = perturbations[0]

    columns = 2 * slot_count
    block = 640
    table, outgoing, odd = pl.pallas_call(
        functools.partial(forward_kernel, slots=slots, block=block),
        in_specs=[WHOLE, WHOLE],
        out_specs=[FAR, WHOLE, WHOLE],
        out_shape=[
            pltpu.HBM((half // LANES, columns, LANES), BF16),
            jax.ShapeDtypeStruct((lat_dev, ROW_HEAD, LANES), BF16),
            jax.ShapeDtypeStruct((8, columns), jnp.int32),
        ],
        scratch_shapes=[
            pltpu.VMEM((LANES, half), BF16),
            pltpu.VMEM((columns, 8), F32),
            pltpu.VMEM((half // LANES, columns, LANES), BF16),
            pltpu.SemaphoreType.DMA((16,)),
        ],
        compiler_params=params(),
        cost_estimate=pl.CostEstimate(flops=10**9, bytes_accessed=7 * 10**6, transcendentals=0),
        name="forward_zonal",
    )(x, wave_map.reshape(1, slot_count))

    incoming = lax.all_to_all(outgoing, "lat", 0, 0, tiled=True)

    row_code = jnp.pad(
        row_map.reshape(lat_dev, rows), ((0, 0), (0, ROW_PAD - rows)), constant_values=-1
    ).reshape(lat_dev * ROW_PAD, 1)
    own = lax.dynamic_slice_in_dim(wave_map, lat * slots, slots)
    own_rows = jnp.tile(own, 4).reshape(4 * slots, 1)
    far_table, band_index = pl.pallas_call(
        functools.partial(prepare_kernel, lat_count=lat_count),
        in_specs=[SCALARS, WHOLE, WHOLE],
        out_specs=[FAR, WHOLE],
        out_shape=[
            pltpu.HBM((lat_dev * ROW_PAD, degrees), BF16),
            jax.ShapeDtypeStruct((4 * slots, degrees), BF16),
        ],
        scratch_shapes=[
            pltpu.VMEM((lat_dev * ROW_PAD, degrees), BF16),
            pltpu.SemaphoreType.DMA((6,)),
        ],
        compiler_params=params(),
        cost_estimate=pl.CostEstimate(flops=10**9, bytes_accessed=4 * 10**6, transcendentals=0),
        name="meridional_table",
    )(cutoffs, row_code, own_rows)

    band_out, power_terms = pl.pallas_call(
        functools.partial(spectral_kernel, slots=slots),
        in_specs=[WHOLE, FAR, WHOLE],
        out_specs=[WHOLE, WHOLE],
        out_shape=[
            jax.ShapeDtypeStruct((lat_dev, 2 * slots, LANES), BF16),
            jax.ShapeDtypeStruct((levels, slots, degrees), F32),
        ],
        scratch_shapes=[pltpu.VMEM(far_table.shape, BF16), pltpu.SemaphoreType.DMA((3,))],
        compiler_params=params(WIDER_LIMIT),
        cost_estimate=pl.CostEstimate(flops=15 * 10**8, bytes_accessed=6 * 10**6, transcendentals=0),
        name="spectral_bands",
    )(incoming, far_table, band_index)

    returned = lax.all_to_all(band_out, "lat", 0, 0, tiled=True).reshape(columns, LANES)
    core, side = mem % 2, mem // 2
    place = jnp.stack([core, side]).astype(jnp.int32)
    lon_dev = lon_count // mem_dev
    share = degrees // mem_dev
    parts = power_terms.reshape(levels, slots, 2, 2, share).transpose(3, 2, 1, 0, 4)
    other = lax.dynamic_index_in_dim(parts, 1 - core, 0, keepdims=False).astype(BF16)
    power = lax.dynamic_index_in_dim(parts, core, 0, keepdims=False) + swap(other, 1).astype(F32)
    other = lax.dynamic_index_in_dim(power, 1 - side, 0, keepdims=False).astype(BF16)
    power = lax.dynamic_index_in_dim(power, side, 0, keepdims=False) + swap(other, 2).astype(F32)
    power = power * (0.5 / (mem_dev - 1))

    lon_dev = lon_count // mem_dev
    kept = levels * rows * bands
    term_rows = 3 * rows * bands
    pair_shape = jax.ShapeDtypeStruct((2, kept, lon_dev), BF16)
    lhs_shape = jax.ShapeDtypeStruct((2 * LANES, columns), BF16)
    place, power = lax.optimization_barrier((place, power))

    near_tiles = 3
    tiles = lon_dev // LANES
    after, _ = lax.optimization_barrier((place, power_terms))
    near_zonal, field = pl.pallas_call(
        functools.partial(fetch_kernel, width=lon_dev),
        in_specs=[SCALARS, WHOLE, FAR],
        out_specs=[WHOLE, WHOLE],
        out_shape=[
            pltpu.VMEM((near_tiles, columns, LANES), BF16),
            pltpu.VMEM((levels * rows, lon_count), F32),
        ],
        scratch_shapes=[pltpu.SemaphoreType.DMA((near_tiles,))],
        compiler_params=params(FETCH_LIMIT),
        cost_estimate=pl.CostEstimate(flops=10**9, bytes_accessed=5 * 10**6, transcendentals=0),
        name="fetch_table",
    )(after, x, table)
    send, lhs, next_zonal = pl.pallas_call(
        inverse_send_kernel,
        in_specs=[SCALARS, WHOLE, WHOLE, WHOLE, WHOLE, FAR],
        out_specs=[WHOLE, WHOLE, WHOLE],
        out_shape=[pair_shape, lhs_shape, pltpu.VMEM((tiles, columns, LANES), BF16)],
        scratch_shapes=[
            pltpu.VMEM((tiles - near_tiles, columns, LANES), BF16),
            pltpu.SemaphoreType.DMA((2 * tiles - near_tiles,)),
        ],
        compiler_params=params(WIDE_LIMIT),
        cost_estimate=pl.CostEstimate(flops=10**9, bytes_accessed=5 * 10**6, transcendentals=0),
        name="inverse_send",
    )(place, returned, odd, field, near_zonal, table)
    came = swap(send, 1)
    keep = pl.pallas_call(
        inverse_keep_kernel,
        in_specs=[SCALARS] + [WHOLE] * 3,
        out_specs=WHOLE,
        out_shape=pair_shape,
        compiler_params=params(),
        cost_estimate=pl.CostEstimate(flops=10**9, bytes_accessed=5 * 10**6, transcendentals=0),
        name="inverse_keep",
    )(place, lhs, field, next_zonal)

    def pair(other, dtype):
        return pl.pallas_call(
            functools.partial(pair_kernel, rows=rows, bands=bands, other=other),
            in_specs=[SCALARS] + [WHOLE] * 2,
            out_specs=WHOLE,
            out_shape=jax.ShapeDtypeStruct((term_rows, lon_dev), dtype),
            compiler_params=params(),
            name="pair_terms",
        )(place, keep, came)

    came_terms = swap(pair(True, BF16), 2)
    band_stats = pl.pallas_call(
        functools.partial(final_kernel, rows=rows, bands=bands, scale=1.0 / (mem_dev - 1)),
        in_specs=[WHOLE, WHOLE],
        out_specs=WHOLE,
        out_shape=jax.ShapeDtypeStruct((3, rows, bands, lon_dev), F32),
        compiler_params=params(),
        name="final_terms",
    )(pair(False, F32), came_terms)
    return (band_stats.transpose(2, 0, 1, 3), power.transpose(1, 2, 0))


def solution(mesh):
    placed = (P("mem", None, "lat", None), P(), P(), P())
    return jax.shard_map(
        shards,
        mesh=mesh,
        in_specs=placed,
        out_specs=(P(None, None, "lat", "mem"), P(None, "mem", "lat")),
        check_vma=False,
    )
```

```python
import functools
import math

import jax
import jax.numpy as jnp
from jax import lax
from jax.experimental import pallas as pl
from jax.experimental.pallas import tpu as pltpu
from jax.sharding import PartitionSpec as P

F32 = jnp.float32
BF16 = jnp.bfloat16
LANES = 128
ROW_PAD = 24
ROW_HEAD = 16
SENT_BANDS = 3
SINE = (
    6.283185307072579,
    -41.341702116996316,
    81.60522620630826,
    -76.70428132156577,
    42.00980565792769,
    -14.394135376685622,
)


def cos_turn(index, period):
    left = index - jnp.round(index * (1.0 / period)) * period
    quarter = 0.25 - jnp.abs(left * (1.0 / period))
    square = quarter * quarter
    total = jnp.full_like(square, SINE[-1])
    for coefficient in SINE[-2::-1]:
        total = total * square + coefficient
    return total * quarter


def cosine_rows(rate, offset, period, weight, steps):
    lane = lax.broadcasted_iota(jnp.int32, (1, LANES), 1).astype(F32)
    start = rate * lane + offset
    stride = rate * float(LANES)
    before = cos_turn(start, period) * weight
    now = cos_turn(start + stride, period) * weight
    twice = jnp.broadcast_to(2.0 * cos_turn(stride, period), before.shape)
    tiles = [before, now]
    while len(tiles) < steps:
        tiles.append(twice * tiles[-1] - tiles[-2])
    return tiles


def move_lanes(block, source, target):
    tile, inner = divmod(source, LANES)
    first = block[:, tile * LANES : (tile + 1) * LANES]
    if inner + 40 > LANES and (tile + 1) * LANES < block.shape[1]:
        second = block[:, (tile + 1) * LANES : (tile + 2) * LANES]
        lane = lax.broadcasted_iota(jnp.int32, first.shape, 1)
        first = jnp.where(lane >= inner, first, second)
    shift = (target - inner) % LANES
    return pltpu.roll(first, shift, 1) if shift else first


def join_lanes(pieces, width):
    lane = lax.broadcasted_iota(jnp.int32, pieces[0].shape, 1)
    out = jnp.zeros_like(pieces[0])
    for index in range(len(pieces) - 1, -1, -1):
        out = jnp.where(lane < (index + 1) * width, pieces[index], out)
    return out


def swap_parts(block, slots):
    rows, lanes = block.shape
    split = block.reshape(rows // (2 * slots), 2 * slots, lanes)
    return pltpu.roll(split, slots, 1).reshape(rows, lanes)


def wave_rows(wave_ref, slots, rows):
    wave = jnp.broadcast_to(wave_ref[...], (rows, wave_ref.shape[1]))
    count = wave.shape[1]
    lane = lax.broadcasted_iota(jnp.int32, (rows, LANES), 1)
    tiles = []
    for tile in range(2 * count // LANES):
        total = jnp.zeros((rows, LANES), jnp.int32)
        first = tile * LANES // slots
        last = ((tile + 1) * LANES - 1) // slots
        for piece in range(first, last + 1):
            device, part = divmod(piece, 2)
            target = piece * slots - tile * LANES
            moved = move_lanes(wave, device * slots, target % LANES)
            mask = jnp.logical_and(lane >= target, lane < target + slots)
            total = jnp.where(mask, moved + 2048 * part, total)
        tiles.append(total)
    return jnp.concatenate(tiles, axis=1)


def forward_kernel(
    x_ref, wave_ref, far_ref, out_ref, odd_ref, folded, sides, table_ref, left, *, slots, block
):
    levels, rows, lon_count = x_ref.shape
    half = lon_count // 2
    columns = table_ref.shape[1]
    period = float(lon_count)

    code = wave_rows(wave_ref, slots, 8)
    part = lax.shift_right_logical(code, 11)
    wave = code - part * 2048
    flags = wave % 2
    odd_ref[...] = flags
    waved = wave.astype(F32)
    phase = part.astype(F32)
    weight = jnp.where(wave == 0, math.sqrt(1.0 / lon_count), math.sqrt(2.0 / lon_count)).astype(F32)
    turn = waved * float(LANES)
    cosine = cos_turn(turn, period)
    sine = cos_turn(turn - 0.25 * period, period) * (2.0 * phase - 1.0)
    index = lax.broadcasted_iota(jnp.int32, code.shape, 0)
    stack = jnp.where(index == 0, waved, -0.25 * period * phase)
    stack = jnp.where(index == 2, weight, stack)
    stack = jnp.where(index == 3, cosine, stack)
    stack = jnp.where(index == 4, sine, stack)
    sides[...] = jnp.transpose(stack)
    folded[...] = jnp.zeros_like(folded)
    for level in range(levels):
        near = x_ref[level, :, :half].astype(F32)
        far = x_ref[level, :, half:].astype(F32)
        folded[32 * level : 32 * level + rows, :] = (near + far).astype(BF16)
        folded[64 + 32 * level : 64 + 32 * level + rows, :] = (near - far).astype(BF16)

    lane = lax.broadcasted_iota(jnp.int32, (1, LANES), 1).astype(F32)
    chunk = 4 * slots

    def make(base, count):
        for start in range(base, base + count, chunk):
            side = sides[start : start + chunk, :]
            now = cos_turn(side[:, 0:1] * lane + side[:, 1:2], period) * side[:, 2:3]
            cosine = jnp.broadcast_to(side[:, 3:4], now.shape)
            later = now * cosine + swap_parts(now, slots) * side[:, 4:5]
            twice = cosine + cosine
            for index in range(half // LANES):
                table_ref[index, start : start + chunk, :] = now.astype(BF16)
                now, later = later, twice * later - now

    width = 2 * slots

    def multiply(base):
        part = jnp.concatenate([table_ref[i, base : base + block, :] for i in range(half // LANES)], axis=1)
        total = lax.dot_general(folded[...], part, (((1,), (1,)), ((), ())), preferred_element_type=F32)
        odd = flags[0:1, base : base + block] == 1
        parts = []
        for level in range(levels):
            low = 32 * level
            parts.append(jnp.where(odd, total[64 + low : 64 + low + 24], total[low : low + 24]))
        rest = parts[0][16:24] + pltpu.roll(parts[1][16:24], 4, 0)
        parts = [part[0:16] for part in parts]
        for dest in range(block // width):
            pieces = [move_lanes(part, dest * width, i * width) for i, part in enumerate(parts)]
            tile = join_lanes(pieces, width)
            last = move_lanes(rest, dest * width, 2 * width)
            where = lax.broadcasted_iota(jnp.int32, last.shape, 1)
            last = jnp.where(jnp.logical_and(where >= 2 * width, where < 3 * width), last, tile[0:8])
            out_ref[base // width + dest] = jnp.concatenate([last, tile[8:16]], axis=0).astype(BF16)

    copies = []
    for base in range(0, columns, block):
        share = columns // left.shape[0]
        for start in range(base, base + block, share):
            make(start, share)
            part = (slice(None), pl.ds(start, share))
            copies.append(pltpu.make_async_copy(table_ref.at[part], far_ref.at[part], left.at[len(copies)]))
            copies[-1].start()
        if base:
            multiply(base - block)
    multiply(columns - block)
    for copy in copies:
        copy.wait()


def prepare_kernel(
    cut_ref, row_ref, own_ref, far_ref, band_ref, table_ref, left, *, lat_count
):
    total, waves = table_ref.shape
    chunk = 64
    lane = lax.broadcasted_iota(jnp.int32, (1, LANES), 1)

    def make(index, carry):
        rows = pl.ds(pl.multiple_of(index * chunk, chunk), chunk)
        row = row_ref[rows, :]
        weight = jnp.where(row < 0, 0.0, math.sqrt(2.0 / lat_count)).astype(F32)
        rate = (2 * row + 1).astype(F32)
        tiles = cosine_rows(rate, 0.0, 4.0 * lat_count, weight, waves // LANES)
        for place, tile in enumerate(tiles):
            if place == 0:
                tile = jnp.where(lane == 0, tile * math.sqrt(0.5), tile)
            table_ref[rows, place * LANES : (place + 1) * LANES] = tile.astype(BF16)
        return carry

    count = left.shape[0]
    size = total // count
    copies = []
    for piece in range(count):
        lax.fori_loop(piece * size // chunk, (piece + 1) * size // chunk, make, 0)
        part = pl.ds(piece * size, size)
        copies.append(pltpu.make_async_copy(table_ref.at[part], far_ref.at[part], left.at[piece]))
        copies[-1].start()
    wave = own_ref[...]
    count = wave.shape[0]
    degree = lax.broadcasted_iota(jnp.int32, (count, waves), 1)
    kappa = degree * degree + wave * wave
    index = jnp.zeros(kappa.shape, F32)
    for i in range(SENT_BANDS):
        index = index + (kappa >= cut_ref[i] * cut_ref[i]).astype(F32)
    band_ref[...] = index.astype(BF16)
    for copy in copies:
        copy.wait()


def spectral_kernel(
    waves_ref, far_ref, band_ref, out_ref, power_ref, table_ref, arrived, *, slots
):
    chunks = arrived.shape[0]
    size = table_ref.shape[0] // chunks
    copies = []
    for chunk in range(chunks):
        part = pl.ds(chunk * size, size)
        copies.append(pltpu.make_async_copy(far_ref.at[part], table_ref.at[part], arrived.at[chunk]))
        copies[-1].start()
    came = waves_ref[...].astype(F32)
    devices = came.shape[0]
    fields = 2 * slots
    count = 2 * fields
    rest = came[:, 0:8, :].reshape(devices * 8, LANES)
    low = pltpu.roll(rest, LANES - count, 1)
    high = pltpu.roll(pltpu.roll(rest, LANES - count + fields, 1).reshape(devices, 8, LANES), 4, 1)
    lane = lax.broadcasted_iota(jnp.int32, high.shape, 2)
    row = lax.broadcasted_iota(jnp.int32, high.shape, 1)
    rest = jnp.where(lane < fields, low.reshape(high.shape), high)
    rest = jnp.where(row < 4, rest, 0.0)
    waves = jnp.concatenate([came, rest], axis=1).reshape(devices * ROW_PAD, LANES).astype(BF16)
    spectra = None
    for chunk in range(chunks):
        copies[chunk].wait()
        term = lax.dot_general(
            waves[chunk * size : (chunk + 1) * size],
            table_ref[pl.ds(chunk * size, size)],
            (((0,), (0,)), ((), ())),
            preferred_element_type=F32,
        )
        spectra = term if spectra is None else spectra + term
    spectra = spectra[0:count, :].astype(BF16)
    wide = spectra.astype(F32)
    square = wide * wide
    for level in range(2):
        base = level * fields
        power_ref[level] = square[base : base + slots, :] + square[base + slots : base + fields, :]
    index = band_ref[...].astype(F32)
    masked = jnp.concatenate(
        [jnp.where(index == float(band), wide, 0.0).astype(BF16) for band in range(SENT_BANDS)], axis=0
    )
    rows = 20
    groups = 4
    share = devices // groups
    wide_rows = share * ROW_PAD
    for group in range(groups):
        band_waves = lax.dot_general(
            masked,
            table_ref[pl.ds(group * wide_rows, wide_rows)],
            (((1,), (1,)), ((), ())),
            preferred_element_type=F32,
        )
        for dest in range(share):
            pieces = []
            for piece in range(2 * SENT_BANDS):
                part = band_waves[piece * fields : (piece + 1) * fields, :]
                pieces.append(move_lanes(part, dest * ROW_PAD, piece * rows))
            out_ref[group * share + dest] = join_lanes(pieces, rows).astype(BF16)


def fetch_kernel(place_ref, x_ref, far_ref, out_ref, field_ref, arrived, *, width):
    first = (1 - place_ref[0]) * (width // LANES)
    copies = []
    for tile in range(out_ref.shape[0]):
        copies.append(pltpu.make_async_copy(far_ref.at[first + tile], out_ref.at[tile], arrived.at[tile]))
        copies[-1].start()
    levels, rows, lon_count = x_ref.shape
    for level in range(levels):
        field_ref[level * rows : (level + 1) * rows, :] = x_ref[level].astype(F32)
    values = field_ref[...]
    lane = lax.broadcasted_iota(jnp.int32, values.shape, 1)
    sign = 1.0 - 2.0 * (lane % 2).astype(F32)
    mean = jnp.sum(values * sign, axis=1, keepdims=True) * (1.0 / lon_count)
    field_ref[...] = values - mean * sign
    for copy in copies:
        copy.wait()


def beside(ref, start, stop):
    return jnp.concatenate([ref[tile] for tile in range(start, stop)], axis=1)


def put_fields(both, field_ref, out_ref, base, start):
    kept, lon_count = field_ref.shape
    width = both.shape[1]
    even, odd = both[:LANES], both[LANES:]
    for side in range(2):
        bands = even + odd if side == 0 else even - odd
        bands = bands.astype(BF16).astype(F32)
        first = pl.multiple_of(base + start + side * (lon_count // 2), LANES)
        rest = field_ref[:, pl.ds(first, width)]
        for band in range(SENT_BANDS):
            rest = rest - bands[band * kept : (band + 1) * kept]
        full = jnp.concatenate([bands[: SENT_BANDS * kept], rest], axis=0).astype(BF16)
        out_ref[side, :, start : start + width] = full


def inverse_send_kernel(
    place_ref, waves_ref, odd_ref, field_ref, near_ref, far_ref, out_ref, lhs, next_ref, last, arrived
):
    width = out_ref.shape[2]
    core = place_ref[0]
    base = pl.multiple_of((1 - core) * width, LANES)
    tiles = width // LANES
    near = near_ref.shape[0]
    ends = []
    for tile in range(near, tiles):
        source = far_ref.at[(1 - core) * tiles + tile]
        ends.append(pltpu.make_async_copy(source, last.at[tile - near], arrived.at[len(ends)]))
    for tile in range(tiles):
        source = far_ref.at[core * tiles + tile]
        ends.append(pltpu.make_async_copy(source, next_ref.at[tile], arrived.at[len(ends)]))
    for copy in ends:
        copy.start()
    waves = jnp.transpose(waves_ref[...].astype(F32))
    odd = waves * odd_ref[0:1, :].astype(F32)
    lhs[0:LANES, :] = (waves - odd).astype(BF16)
    lhs[LANES:, :] = odd.astype(BF16)
    both = jnp.dot(lhs[...], beside(near_ref, 0, near), preferred_element_type=F32)
    put_fields(both, field_ref, out_ref, base, 0)
    for copy in ends[: tiles - near]:
        copy.wait()
    both = jnp.dot(lhs[...], beside(last, 0, tiles - near), preferred_element_type=F32)
    put_fields(both, field_ref, out_ref, base, near * LANES)
    for copy in ends[tiles - near :]:
        copy.wait()


def inverse_keep_kernel(place_ref, lhs, field_ref, table_ref, out_ref):
    width = out_ref.shape[2]
    base = pl.multiple_of(place_ref[0] * width, LANES)
    for start in range(0, width, 256):
        stop = min(start + 256, width)
        part = beside(table_ref, start // LANES, stop // LANES)
        both = jnp.dot(lhs[...], part, preferred_element_type=F32)
        put_fields(both, field_ref, out_ref, base, start)


def terms_of(first, second, rows, bands):
    a, b = first.astype(F32), second.astype(F32)
    cross = []
    for band in range(bands):
        low = band * 2 * rows
        mid, high = low + rows, low + 2 * rows
        cross.append(a[low:mid] * a[mid:high] + b[low:mid] * b[mid:high])
    return [a * a + b * b] + cross


def pair_kernel(place_ref, keep_ref, came_ref, out_ref, *, rows, bands, other):
    which = 1 - place_ref[1] if other else place_ref[1]
    pieces = terms_of(keep_ref[which], came_ref[which], rows, bands)
    out_ref[...] = jnp.concatenate(pieces, axis=0).astype(out_ref.dtype)


def final_kernel(own_ref, came_ref, out_ref, *, rows, bands, scale):
    wide = 2 * rows * bands
    total = own_ref[...] + came_ref[...].astype(F32)
    stats = total[: 3 * rows * bands] * scale
    for band in range(bands):
        low = band * 2 * rows
        out_ref[0, :, band, :] = stats[low : low + rows]
        out_ref[1, :, band, :] = stats[low + rows : low + 2 * rows]
        out_ref[2, :, band, :] = stats[wide + band * rows : wide + (band + 1) * rows]


VMEM_LIMIT = 24 * 1024 * 1024
WIDE_LIMIT = 44_000_000
FETCH_LIMIT = 54_000_000
WIDER_LIMIT = 54_000_000
WHOLE = pl.BlockSpec(memory_space=pltpu.VMEM)
FAR = pl.BlockSpec(memory_space=pltpu.HBM)
SCALARS = pl.BlockSpec(memory_space=pltpu.SMEM)


def params(limit=VMEM_LIMIT):
    return pltpu.CompilerParams(vmem_limit_bytes=limit)


def shards(perturbations, row_map, wave_map, cutoffs):
    _, levels, rows, lon_count = perturbations.shape
    lat_dev = lax.axis_size("lat")
    mem_dev = lax.axis_size("mem")
    lat = lax.axis_index("lat")
    mem = lax.axis_index("mem")
    swap = lambda value, bit: lax.ppermute(value, "mem", [(i, i ^ bit) for i in range(mem_dev)])
    lat_count = rows * lat_dev
    slot_count = wave_map.shape[0]
    slots = slot_count // lat_dev
    degrees = row_map.shape[0]
    bands = cutoffs.shape[0] + 1
    half = lon_count // 2
    x = perturbations[0]

    columns = 2 * slot_count
    block = 1280
    table, outgoing, odd = pl.pallas_call(
        functools.partial(forward_kernel, slots=slots, block=block),
        in_specs=[WHOLE, WHOLE],
        out_specs=[FAR, WHOLE, WHOLE],
        out_shape=[
            pltpu.HBM((half // LANES, columns, LANES), BF16),
            jax.ShapeDtypeStruct((lat_dev, ROW_HEAD, LANES), BF16),
            jax.ShapeDtypeStruct((8, columns), jnp.int32),
        ],
        scratch_shapes=[
            pltpu.VMEM((LANES, half), BF16),
            pltpu.VMEM((columns, 8), F32),
            pltpu.VMEM((half // LANES, columns, LANES), BF16),
            pltpu.SemaphoreType.DMA((16,)),
        ],
        compiler_params=params(),
        cost_estimate=pl.CostEstimate(flops=10**9, bytes_accessed=7 * 10**6, transcendentals=0),
        name="forward_zonal",
    )(x, wave_map.reshape(1, slot_count))

    incoming = lax.all_to_all(outgoing, "lat", 0, 0, tiled=True)

    row_code = jnp.pad(
        row_map.reshape(lat_dev, rows), ((0, 0), (0, ROW_PAD - rows)), constant_values=-1
    ).reshape(lat_dev * ROW_PAD, 1)
    own = lax.dynamic_slice_in_dim(wave_map, lat * slots, slots)
    own_rows = jnp.tile(own, 4).reshape(4 * slots, 1)
    far_table, band_index = pl.pallas_call(
        functools.partial(prepare_kernel, lat_count=lat_count),
        in_specs=[SCALARS, WHOLE, WHOLE],
        out_specs=[FAR, WHOLE],
        out_shape=[
            pltpu.HBM((lat_dev * ROW_PAD, degrees), BF16),
            jax.ShapeDtypeStruct((4 * slots, degrees), BF16),
        ],
        scratch_shapes=[
            pltpu.VMEM((lat_dev * ROW_PAD, degrees), BF16),
            pltpu.SemaphoreType.DMA((6,)),
        ],
        compiler_params=params(),
        cost_estimate=pl.CostEstimate(flops=10**9, bytes_accessed=4 * 10**6, transcendentals=0),
        name="meridional_table",
    )(cutoffs, row_code, own_rows)

    band_out, power_terms = pl.pallas_call(
        functools.partial(spectral_kernel, slots=slots),
        in_specs=[WHOLE, FAR, WHOLE],
        out_specs=[WHOLE, WHOLE],
        out_shape=[
            jax.ShapeDtypeStruct((lat_dev, 2 * slots, LANES), BF16),
            jax.ShapeDtypeStruct((levels, slots, degrees), F32),
        ],
        scratch_shapes=[pltpu.VMEM(far_table.shape, BF16), pltpu.SemaphoreType.DMA((3,))],
        compiler_params=params(WIDER_LIMIT),
        cost_estimate=pl.CostEstimate(flops=15 * 10**8, bytes_accessed=6 * 10**6, transcendentals=0),
        name="spectral_bands",
    )(incoming, far_table, band_index)

    returned = lax.all_to_all(band_out, "lat", 0, 0, tiled=True).reshape(columns, LANES)
    core, side = mem % 2, mem // 2
    place = jnp.stack([core, side]).astype(jnp.int32)
    lon_dev = lon_count // mem_dev
    share = degrees // mem_dev
    parts = power_terms.reshape(levels, slots, 2, 2, share).transpose(3, 2, 1, 0, 4)
    other = lax.dynamic_index_in_dim(parts, 1 - core, 0, keepdims=False).astype(BF16)
    power = lax.dynamic_index_in_dim(parts, core, 0, keepdims=False) + swap(other, 1).astype(F32)
    other = lax.dynamic_index_in_dim(power, 1 - side, 0, keepdims=False).astype(BF16)
    power = lax.dynamic_index_in_dim(power, side, 0, keepdims=False) + swap(other, 2).astype(F32)
    power = power * (0.5 / (mem_dev - 1))

    lon_dev = lon_count // mem_dev
    kept = levels * rows * bands
    term_rows = 3 * rows * bands
    pair_shape = jax.ShapeDtypeStruct((2, kept, lon_dev), BF16)
    lhs_shape = jax.ShapeDtypeStruct((2 * LANES, columns), BF16)
    place, power = lax.optimization_barrier((place, power))

    near_tiles = 3
    tiles = lon_dev // LANES
    after, _ = lax.optimization_barrier((place, power_terms))
    near_zonal, field = pl.pallas_call(
        functools.partial(fetch_kernel, width=lon_dev),
        in_specs=[SCALARS, WHOLE, FAR],
        out_specs=[WHOLE, WHOLE],
        out_shape=[
            pltpu.VMEM((near_tiles, columns, LANES), BF16),
            pltpu.VMEM((levels * rows, lon_count), F32),
        ],
        scratch_shapes=[pltpu.SemaphoreType.DMA((near_tiles,))],
        compiler_params=params(FETCH_LIMIT),
        cost_estimate=pl.CostEstimate(flops=10**9, bytes_accessed=5 * 10**6, transcendentals=0),
        name="fetch_table",
    )(after, x, table)
    send, lhs, next_zonal = pl.pallas_call(
        inverse_send_kernel,
        in_specs=[SCALARS, WHOLE, WHOLE, WHOLE, WHOLE, FAR],
        out_specs=[WHOLE, WHOLE, WHOLE],
        out_shape=[pair_shape, lhs_shape, pltpu.VMEM((tiles, columns, LANES), BF16)],
        scratch_shapes=[
            pltpu.VMEM((tiles - near_tiles, columns, LANES), BF16),
            pltpu.SemaphoreType.DMA((2 * tiles - near_tiles,)),
        ],
        compiler_params=params(WIDE_LIMIT),
        cost_estimate=pl.CostEstimate(flops=10**9, bytes_accessed=5 * 10**6, transcendentals=0),
        name="inverse_send",
    )(place, returned, odd, field, near_zonal, table)
    came = swap(send, 1)
    keep = pl.pallas_call(
        inverse_keep_kernel,
        in_specs=[SCALARS] + [WHOLE] * 3,
        out_specs=WHOLE,
        out_shape=pair_shape,
        compiler_params=params(),
        cost_estimate=pl.CostEstimate(flops=10**9, bytes_accessed=5 * 10**6, transcendentals=0),
        name="inverse_keep",
    )(place, lhs, field, next_zonal)

    def pair(other, dtype):
        return pl.pallas_call(
            functools.partial(pair_kernel, rows=rows, bands=bands, other=other),
            in_specs=[SCALARS] + [WHOLE] * 2,
            out_specs=WHOLE,
            out_shape=jax.ShapeDtypeStruct((term_rows, lon_dev), dtype),
            compiler_params=params(),
            name="pair_terms",
        )(place, keep, came)

    came_terms = swap(pair(True, BF16), 2)
    band_stats = pl.pallas_call(
        functools.partial(final_kernel, rows=rows, bands=bands, scale=1.0 / (mem_dev - 1)),
        in_specs=[WHOLE, WHOLE],
        out_specs=WHOLE,
        out_shape=jax.ShapeDtypeStruct((3, rows, bands, lon_dev), F32),
        compiler_params=params(),
        name="final_terms",
    )(pair(False, F32), came_terms)
    return (band_stats.transpose(2, 0, 1, 3), power.transpose(1, 2, 0))


def solution(mesh):
    placed = (P("mem", None, "lat", None), P(), P(), P())
    return jax.shard_map(
        shards,
        mesh=mesh,
        in_specs=placed,
        out_specs=(P(None, None, "lat", "mem"), P(None, "mem", "lat")),
        check_vma=False,
    )
```
